256 devices in a mesh: dp: 2 (over x_lo), ctx: 128 (over z, y, x_hi, core).
Axes of the slice: x: 4 (x_hi: 2, x_lo: 2; x = x_hi * 2 + x_lo), y: 4, z: 8, core: 2. Of those that a mesh axis runs over, the one named last changes fastest.
Arguments:
- value_rows: bfloat16 [16384, 4096], P('ctx', 'dp'), may hold values from -6 to 6
- gate_rows: bfloat16 [16384, 4096], P('ctx', 'dp'), may hold values from -400 to 400
- filter_rows: bfloat16 [16384, 256], P('ctx', 'dp'), may hold values from -0.046875 to 0.046875
- skip: float32 [4096], P('dp'), may hold values from -4 to 4
- old_owner: int32 [128], replicated, may hold values from 0 to 127, each once
- new_owner: int32 [128], replicated, may hold values from 0 to 127, each once
Outputs:
- mixed_rows: bfloat16 [16384, 4096], P('ctx', 'dp')
The draws below stay inside these ranges and needn't reach their ends.
Inputs may be any that keep to these rules, and one draw needn't show every extreme that they name: `old_owner`: a permutation of the indices of ctx. `new_owner`: a permutation of the indices of ctx.
All inputs are finite; a program needn't handle non-finite values.
Results may differ from the reference program's by a relative error of at most 0.0095.
Values may be sent and summed in bfloat16 or wider, within the bound.
A program may use at most 64 MiB of HBM per device.

```python
import math
import jax
import jax.numpy as jnp
from jax import lax

ROWS = 128
CH = 4096
GROUP = 16
BLOCKS = 128
SEQ = 16384


def draw_gate_rows(key, part):
    key = jax.random.fold_in(key, 7)
    jitter_key, row_key = jax.random.split(key)
    column_ramp = jnp.arange(CH, dtype=jnp.float32) / CH
    jitter = jnp.clip(jax.random.normal(jitter_key, (SEQ, CH), jnp.float32), -4.0, 4.0)
    column_scale = jnp.power(10.0, column_ramp)
    row_scale = jnp.power(10.0, jax.random.uniform(row_key, (SEQ, 1), jnp.float32))
    return (jitter * row_scale * column_scale[None, :]).astype(jnp.bfloat16)


def block_scale(rng, dims, pieces, least, top_value):
    def one(dim, parts):
        draws = jax.random.uniform(jax.random.fold_in(jax.random.fold_in(rng, 6), dim), (parts,), jnp.float32, least / len(pieces), top_value / len(pieces))
        return jnp.repeat(jnp.exp(draws), dims[dim] // parts).reshape((-1,) + (1,) * (len(dims) - dim - 1))

    loudness = one(*pieces[0])
    for cut in pieces[1:]:
        loudness = loudness * one(*cut)
    return loudness


def noise(own_key, extent, width, limit, pieces=(), kind=jnp.bfloat16):
    values = width * jax.random.normal(own_key, extent, jnp.float32)
    if pieces:
        values = values * block_scale(own_key, extent, pieces, -0.22, 0.18)
    return jnp.clip(values, -limit, limit).astype(kind)


def setup_inputs(seed: int = 0) -> dict:
    splits = jax.random.split(jax.random.key(seed), 7)
    value_rows = noise(splits[0], (SEQ, CH), 1.0, 6.0, ((0, 128), (1, 2)))
    gate_rows = draw_gate_rows(jax.random.fold_in(splits[6], 71), 0)
    filter_rows = noise(splits[2], (SEQ, CH // GROUP), SEQ ** -0.5, 0.046875, ((0, 128), (1, 2)))
    skip = noise(splits[3], (CH,), 1.0, 4.0, ((0, 2),), jnp.float32)
    old_owner = jax.random.permutation(splits[4], BLOCKS).astype(jnp.int32)
    new_owner = jax.random.permutation(splits[5], BLOCKS).astype(jnp.int32)
    return {"value_rows": value_rows, "gate_rows": gate_rows, "filter_rows": filter_rows, "skip": skip, "old_owner": old_owner, "new_owner": new_owner}


def twiddle_pair(indices, period):
    wrapped = indices % period
    mirror = jnp.minimum(wrapped, period - wrapped)
    angles = mirror.astype(jnp.float32) * (2.0 * math.pi / period)
    sines = jnp.where((mirror == 0) | (2 * mirror == period), jnp.zeros_like(angles), jnp.sin(angles))
    sines = jnp.where(wrapped > period - wrapped, -sines, sines)
    return (jnp.cos(angles), -sines)

def rounded(values):
    return lax.optimization_barrier(values.astype(jnp.bfloat16)).astype(jnp.float32)

def reference(value_rows, gate_rows, filter_rows, skip, old_owner, new_owner):
    period = 2 * BLOCKS
    full_length = 2 * SEQ
    values = value_rows.reshape(BLOCKS, ROWS, CH)[old_owner].astype(jnp.float32)
    gates = gate_rows.reshape(BLOCKS, ROWS, CH)[old_owner].astype(jnp.float32)
    taps = filter_rows.reshape(BLOCKS, ROWS, CH // GROUP).astype(jnp.float32)
    lanes = jnp.arange(BLOCKS, dtype=jnp.int32)
    spots = jnp.arange(ROWS, dtype=jnp.int32)
    dft_re, dft_im = twiddle_pair(spots[:, None] * spots[None, :], ROWS)
    dft_re = rounded(dft_re)
    dft_im = rounded(dft_im)
    highest = lax.Precision.HIGHEST

    def pair_step(mixed, position):
        partner = jnp.where(position == 0, BLOCKS, period - position).astype(jnp.int32)
        columns = jnp.stack([position, partner])
        tab_re, tab_im = twiddle_pair(lanes[:, None] * columns[None, :], period)
        tab_re = rounded(tab_re)
        tab_im = rounded(tab_im)
        turn_re, turn_im = twiddle_pair(columns[:, None] * spots[None, :], full_length)
        turn_re = turn_re[:, :, None]
        turn_im = turn_im[:, :, None]

        def spectrum(inputs):
            part_re = rounded(jnp.einsum('aj,aqx->jqx', tab_re, inputs, precision=highest))
            part_im = rounded(jnp.einsum('aj,aqx->jqx', tab_im, inputs, precision=highest))
            turned_re = rounded(turn_re * part_re - turn_im * part_im)
            turned_im = rounded(turn_re * part_im + turn_im * part_re)
            out_re = jnp.einsum('bd,jbx->jdx', dft_re, turned_re, precision=highest) - jnp.einsum('bd,jbx->jdx', dft_im, turned_im, precision=highest)
            out_im = jnp.einsum('bd,jbx->jdx', dft_re, turned_im, precision=highest) + jnp.einsum('bd,jbx->jdx', dft_im, turned_re, precision=highest)
            return (out_re, out_im)
        value_spec_re, value_spec_im = spectrum(values)
        group_spec_re, group_spec_im = spectrum(taps)
        filter_spec_re = jnp.repeat(group_spec_re, GROUP, axis=2)
        filter_spec_im = jnp.repeat(group_spec_im, GROUP, axis=2)
        prod_re = rounded(value_spec_re * filter_spec_re - value_spec_im * filter_spec_im)
        prod_im = rounded(value_spec_re * filter_spec_im + value_spec_im * filter_spec_re)
        inner_re = jnp.einsum('bd,jdx->jbx', dft_re, prod_re, precision=highest) + jnp.einsum('bd,jdx->jbx', dft_im, prod_im, precision=highest)
        inner_im = jnp.einsum('bd,jdx->jbx', dft_re, prod_im, precision=highest) - jnp.einsum('bd,jdx->jbx', dft_im, prod_re, precision=highest)
        back_re = rounded(turn_re * inner_re + turn_im * inner_im)
        back_im = rounded(turn_re * inner_im - turn_im * inner_re)
        term = jnp.einsum('aj,jqx->aqx', tab_re, back_re, precision=highest) + jnp.einsum('aj,jqx->aqx', tab_im, back_im, precision=highest)
        return (mixed + term, None)
    start = jnp.zeros((BLOCKS, ROWS, CH), jnp.float32)
    mixed, unused = lax.scan(pair_step, start, lanes)
    mixed = mixed / full_length
    gated = gates * (mixed + skip * values)
    squares = lax.optimization_barrier(jnp.sum(gated * gated, axis=2, keepdims=True))
    normed = (gated * lax.rsqrt(squares / CH + 1e-05)).astype(jnp.bfloat16)
    placed = jnp.zeros_like(normed).at[new_owner].set(normed)
    return placed.reshape(SEQ, CH)
```

```python
import functools
import math

import jax
import jax.numpy as jnp
import numpy as np
from jax import lax
from jax.experimental import pallas as pl
from jax.experimental.pallas import tpu as pltpu
from jax.sharding import PartitionSpec as P

MESH = pl.DeviceIdType.MESH
F32 = jnp.float32
BF16 = jnp.bfloat16


def twist(indices, period):
    wrapped = indices % period
    mirror = np.minimum(wrapped, period - wrapped)
    angles = mirror.astype(np.float64) * (2.0 * math.pi / period)
    sines = np.where((mirror == 0) | (2 * mirror == period), 0.0, np.sin(angles))
    sines = np.where(wrapped > period - wrapped, -sines, sines)
    return np.cos(angles), -sines


def make_tables(blocks, rows):
    period, full = 2 * blocks, 2 * blocks * rows
    a, b = np.arange(blocks), np.arange(rows)
    re, im = twist(a[:, None] * a[None, :], period)
    edge = twist(np.full((1, 1), blocks) * a[None, :], period)[0]
    im[:1] = edge
    first = np.concatenate([re, im], axis=0)
    weight = np.full((blocks, 1), 2.0 / full)
    weight[0] = 1.0 / full
    last = np.concatenate([re * weight, im * weight], axis=0)
    turn_re, turn_im = twist(a[:, None] * b[None, :], full)
    edge_re, edge_im = twist(blocks * b[None, :], full)
    dre, dim = twist(b[:, None] * b[None, :], rows)
    fwd = np.block([[dre, dim], [-dim, dre]])
    inv = np.block([[dre, -dim], [dim, dre]])
    low = lambda t: np.asarray(t, np.float32).astype(jnp.bfloat16)
    wide = lambda t: np.asarray(t, np.float32)
    return (
        low(first),
        low(last.T),
        low(fwd),
        low(inv),
        np.stack([wide(turn_re), wide(turn_im)]),
        np.concatenate([wide(edge_re), wide(edge_im)], axis=0),
    )


def transposed(tile):
    return tile.astype(F32).T


def dot(x, y):
    return jnp.dot(x, y, preferred_element_type=F32)


def kernel(
    blocks, group, sizes,
    route_ref, skip_ref, value_ref, gate_ref, filter_ref, old_ref, new_ref,
    first_ref, last_ref, fwd_ref, inv_ref, turn_ref, edge_ref,
    out_ref,
    send_v, send_g, send_f, got_v, got_g, got_f, send_o, got_o,
    wide, lanes, turned, back, conv, edges, sums, partner_sums,
    send_sem, recv_sem,
):
    me = lax.axis_index("ctx")
    half = lax.axis_index("dp")
    rows = value_ref.shape[0]
    channels = value_ref.shape[1]
    per_tile = 128 // group
    nz, ny, nx = sizes

    def peer(k):
        nc = 2
        z = me // (ny * nx * nc)
        y = (me // (nx * nc)) % ny
        x = (me // nc) % nx
        c = me % nc
        dz = k % nz
        r = k // nz
        dy = r % ny
        dx = (r // ny) % nx
        dc = r // (ny * nx)
        return (((z + dz) % nz * ny + (y + dy) % ny) * nx + (x + dx) % nx) * nc + (c + dc) % nc

    barrier = pltpu.get_barrier_semaphore()

    def greet(k, carry):
        pl.semaphore_signal(
            barrier, inc=1, device_id={"ctx": lax.rem(me + k, blocks)}, device_id_type=MESH
        )
        return carry

    lax.fori_loop(1, blocks, greet, 0)
    pl.semaphore_signal(barrier, inc=1, device_id={"dp": 1 - half}, device_id_type=MESH)

    for tile in range(channels // 128):
        at = slice(tile * 128, tile * 128 + 128)
        to = slice(tile * per_tile, tile * per_tile + per_tile)
        send_v[to] = transposed(value_ref[:, at]).astype(BF16).reshape(per_tile, group, rows)
        send_g[to] = transposed(gate_ref[:, at]).astype(BF16).reshape(per_tile, group, rows)
    send_f[...] = transposed(filter_ref[...]).reshape(blocks, 1, rows)
    got_v[me] = send_v[me]
    got_g[me] = send_g[me]
    got_f[me] = send_f[me]

    pl.semaphore_wait(barrier, blocks)

    def remote(src, dst, index, to):
        return pltpu.make_async_remote_copy(
            src_ref=src, dst_ref=dst, send_sem=send_sem.at[index], recv_sem=recv_sem.at[index],
            device_id=to, device_id_type=MESH,
        )

    def all_of(src, dst, index):
        rest = pl.ds(0, blocks - 1)
        return remote(src.at[rest], dst.at[rest], index, {"dp": 1 - half})

    def send_first(k, carry):
        to = peer(k)
        remote(send_v.at[to], got_v.at[me], 0, {"ctx": to}).start()
        remote(send_f.at[to], got_f.at[me], 1, {"ctx": to}).start()
        return carry

    lax.fori_loop(1, blocks, send_first, 0)

    def send_gates(k, carry):
        to = peer(k)
        remote(send_g.at[to], got_g.at[me], 2, {"ctx": to}).start()
        return carry

    lax.fori_loop(1, blocks, send_gates, 0)

    spot = lax.broadcasted_iota(jnp.int32, (blocks, blocks), 0)
    hot_old = jnp.where(old_ref[...] == spot, 1.0, 0.0).astype(BF16)
    hot_new = jnp.where(new_ref[...] == spot, 1.0, 0.0).astype(BF16)
    first_slots = lax.dot_general(
        first_ref[...], hot_old, (((1,), (1,)), ((), ())), preferred_element_type=F32
    ).astype(BF16)
    last_slots = dot(hot_new, last_ref[...]).astype(BF16)

    turn_re, turn_im = turn_ref[0], turn_ref[1]
    edge_re, edge_im = edge_ref[0:1], edge_ref[1:2]
    top = lax.broadcasted_iota(jnp.int32, (blocks, rows), 0) == 0

    def turn(part, unit):
        part = part.astype(BF16).astype(F32)
        re, im = part[:blocks], part[blocks:]
        edges[pl.ds(unit, 1), :] = im[0:1]
        im = jnp.where(top, 0.0, im)
        at = pl.ds(unit * blocks, blocks)
        turned[at, :rows] = (turn_re * re - turn_im * im).astype(BF16)
        turned[at, rows:] = (turn_re * im + turn_im * re).astype(BF16)

    edges[...] = jnp.zeros_like(edges)
    all_of(send_v, got_v, 0).wait_recv()
    wide[...] = got_v[...].astype(F32).reshape(blocks * group, rows)
    for h in range(group):
        lanes[:, h * rows:(h + 1) * rows] = wide[pl.ds(h, blocks, stride=group), :].astype(BF16)
    for h in range(0, group, 2):
        part = dot(first_slots, lanes[:, h * rows:(h + 2) * rows])
        turn(part[:, :rows], h)
        turn(part[:, rows:], h + 1)
    all_of(send_f, got_f, 1).wait_recv()
    taps = got_f[...].reshape(blocks, rows).astype(BF16)
    turn(dot(first_ref[...], taps), group)

    fwd = fwd_ref[...]
    inv = inv_ref[...]
    filt = dot(turned[group * blocks:(group + 1) * blocks], fwd)
    filt_re, filt_im = filt[:, :rows], filt[:, rows:]
    line = edges[...]
    edge_spec = dot(
        jnp.concatenate([(edge_re * line).astype(BF16), (edge_im * line).astype(BF16)], axis=1), fwd
    )

    def multiplied(spec, fre, fim):
        re, im = spec[:, :rows], spec[:, rows:]
        return jnp.concatenate(
            [(re * fre - im * fim).astype(BF16), (re * fim + im * fre).astype(BF16)], axis=1
        )

    edge_filt = edge_spec[group:group + 1]
    edge_inner = dot(multiplied(edge_spec, edge_filt[:, :rows], edge_filt[:, rows:]), inv)
    edges[...] = edge_re * edge_inner[:, :rows] + edge_im * edge_inner[:, rows:]

    for h in range(0, group, 2):
        spec = dot(turned[h * blocks:(h + 2) * blocks], fwd)
        prod = jnp.concatenate(
            [multiplied(spec[:blocks], filt_re, filt_im), multiplied(spec[blocks:], filt_re, filt_im)],
            axis=0,
        )
        inner = dot(prod, inv)
        for i in range(2):
            re = inner[i * blocks:(i + 1) * blocks, :rows]
            im = inner[i * blocks:(i + 1) * blocks, rows:]
            back_im = jnp.where(top, edges[h + i:h + i + 1, :], turn_re * im - turn_im * re)
            at = slice(i * rows, (i + 1) * rows)
            back[:blocks, at] = (turn_re * re + turn_im * im).astype(BF16)
            back[blocks:, at] = back_im.astype(BF16)
        mixed = dot(last_slots, back[...])
        conv[pl.ds(h, blocks, stride=group), :] = mixed[:, :rows]
        conv[pl.ds(h + 1, blocks, stride=group), :] = mixed[:, rows:]

    mine = skip_ref[pl.ds(me, 1), :]
    square = lax.broadcasted_iota(jnp.int32, (group, group), 0) == lax.broadcasted_iota(
        jnp.int32, (group, group), 1
    )
    skips = jnp.sum(jnp.where(square, mine, 0.0), axis=1, keepdims=True)

    all_of(send_g, got_g, 2).wait_recv()

    def gate(to):
        slot = route_ref[to]
        tile = conv[pl.ds(pl.multiple_of(to * group, group), group), :]
        values = got_v[slot].astype(F32)
        return (got_g[slot].astype(F32) * (tile + skips * values)).astype(BF16)

    def send_out(k, carry):
        to = peer(k)
        send_o[to] = gate(to)
        remote(send_o.at[to], got_o.at[me], 3, {"ctx": to}).start()
        return carry

    got_o[me] = gate(me)
    lax.fori_loop(1, blocks, send_out, 0)
    all_of(send_v, got_v, 0).wait_send()
    all_of(send_f, got_f, 1).wait_send()
    all_of(send_g, got_g, 2).wait_send()
    all_of(send_o, got_o, 3).wait_recv()

    full = got_o[...].astype(F32).reshape(blocks * group, rows)
    sums[...] = jnp.broadcast_to(jnp.sum(full * full, axis=0, keepdims=True), sums.shape)
    swap = remote(sums, partner_sums, 4, {"dp": 1 - half})
    swap.start()
    swap.wait()
    scale = lax.rsqrt((sums[0:1] + partner_sums[0:1]) / (2 * channels) + 1e-05)
    for tile in range(channels // 128):
        piece = got_o[tile * per_tile:(tile + 1) * per_tile].astype(F32).reshape(128, rows)
        out_ref[:, tile * 128:(tile + 1) * 128] = (piece * scale).T.astype(BF16)
    all_of(send_o, got_o, 3).wait_send()


def body(sizes, value_rows, gate_rows, filter_rows, skip, old_owner, new_owner):
    blocks = lax.axis_size("ctx")
    rows, channels = value_rows.shape
    group = channels // blocks
    tables = [jnp.asarray(t) for t in make_tables(blocks, rows)]
    lanes = jnp.arange(blocks, dtype=jnp.int32)
    route = jnp.sum(jnp.where(new_owner[:, None] == lanes[None, :], old_owner[:, None], 0), axis=0)
    vmem = pl.BlockSpec(memory_space=pltpu.VMEM)
    smem = pl.BlockSpec(memory_space=pltpu.SMEM)
    slots = pltpu.VMEM((blocks, group, rows), BF16)
    lines = pltpu.VMEM((blocks, 1, rows), F32)
    return pl.pallas_call(
        functools.partial(kernel, blocks, group, sizes),
        out_shape=jax.ShapeDtypeStruct((rows, channels), BF16),
        in_specs=[smem] + [vmem] * 12,
        out_specs=vmem,
        scratch_shapes=[
            slots, slots, lines, slots, slots, lines, slots, slots,
            pltpu.VMEM((blocks * group, rows), F32),
            pltpu.VMEM((blocks, group * rows), BF16),
            pltpu.VMEM(((group + 1) * blocks, 2 * rows), BF16),
            pltpu.VMEM((2 * blocks, 2 * rows), BF16),
            pltpu.VMEM((blocks * group, rows), F32),
            pltpu.VMEM((group + 16, rows), F32),
            pltpu.VMEM((8, rows), F32),
            pltpu.VMEM((8, rows), F32),
            pltpu.SemaphoreType.DMA((5,)),
            pltpu.SemaphoreType.DMA((5,)),
        ],
        compiler_params=pltpu.CompilerParams(
            collective_id=0, has_side_effects=True, vmem_limit_bytes=48 << 20
        ),
    )(
        route, skip.reshape(blocks, group), value_rows, gate_rows, filter_rows,
        old_owner.reshape(1, blocks), new_owner.reshape(1, blocks), *tables,
    )


def solution(mesh):
    placed = (P("ctx", "dp"), P("ctx", "dp"), P("ctx", "dp"), P("dp"), P(), P())
    sizes = (8, 4, 2)
    return jax.shard_map(
        functools.partial(body, sizes), mesh=mesh, in_specs=placed, out_specs=P("ctx", "dp"), check_vma=False
    )
```

```python
import functools
import math

import jax
import jax.numpy as jnp
import numpy as np
from jax import lax
from jax.experimental import pallas as pl
from jax.experimental.pallas import tpu as pltpu
from jax.sharding import PartitionSpec as P

MESH = pl.DeviceIdType.MESH
F32 = jnp.float32
BF16 = jnp.bfloat16


def twist(indices, period):
    wrapped = indices % period
    mirror = np.minimum(wrapped, period - wrapped)
    angles = mirror.astype(np.float64) * (2.0 * math.pi / period)
    sines = np.where((mirror == 0) | (2 * mirror == period), 0.0, np.sin(angles))
    sines = np.where(wrapped > period - wrapped, -sines, sines)
    return np.cos(angles), -sines


def make_tables(blocks, rows):
    period, full = 2 * blocks, 2 * blocks * rows
    a, b = np.arange(blocks), np.arange(rows)
    re, im = twist(a[:, None] * a[None, :], period)
    edge = twist(np.full((1, 1), blocks) * a[None, :], period)[0]
    im[:1] = edge
    first = np.concatenate([re, im], axis=0)
    weight = np.full((blocks, 1), 2.0 / full)
    weight[0] = 1.0 / full
    last = np.concatenate([re * weight, im * weight], axis=0)
    turn_re, turn_im = twist(a[:, None] * b[None, :], full)
    edge_re, edge_im = twist(blocks * b[None, :], full)
    dre, dim = twist(b[:, None] * b[None, :], rows)
    fwd = np.block([[dre, dim], [-dim, dre]])
    inv = np.block([[dre, -dim], [dim, dre]])
    low = lambda t: np.asarray(t, np.float32).astype(jnp.bfloat16)
    wide = lambda t: np.asarray(t, np.float32)
    return (
        low(first),
        low(np.concatenate([last[:blocks].T, last[blocks:].T], axis=0)),
        low(np.concatenate([fwd[:, :rows], fwd[:, rows:]], axis=0)),
        low(np.concatenate([inv[:, :rows], inv[:, rows:]], axis=0)),
        np.stack([wide(turn_re), wide(turn_im)]),
        np.concatenate([wide(edge_re), wide(edge_im)], axis=0),
    )


def transposed(tile):
    return tile.astype(F32).T


def beside(ref):
    depth = ref.shape[0] // 2
    return jnp.concatenate([ref[:depth], ref[depth:]], axis=1)


def dot(x, y):
    return jnp.dot(x, y, preferred_element_type=F32)


def kernel(
    blocks, group, sizes,
    skip_ref, value_hbm, gate_hbm, filter_hbm, old_hbm, new_hbm,
    first_hbm, last_hbm, fwd_hbm, inv_hbm, turn_hbm, edge_hbm,
    out_hbm, scale_ref, out_ref,
    value_ref, gate_ref, filter_ref, old_ref, new_ref,
    first_ref, last_ref, fwd_ref, inv_ref, turn_ref, edge_ref,
    send_v, send_g, send_f, got_v, got_g, got_f, send_o, got_o,
    wide, lanes, turned, back, conv, edges, sums, partner_sums, route_row, route_ref,
    load_sem, send_sem, recv_sem,
):
    me = lax.axis_index("ctx")
    half = lax.axis_index("dp")
    rows, channels = value_ref.shape
    per_tile = 128 // group
    nz, ny, nx, nc = sizes
    low = ny * nx * nc

    loads = [
        pltpu.make_async_copy(src, dst, load_sem.at[i])
        for i, (src, dst) in enumerate([
            (value_hbm, value_ref), (filter_hbm, filter_ref), (gate_hbm, gate_ref),
            (old_hbm, old_ref), (new_hbm, new_ref), (first_hbm, first_ref), (last_hbm, last_ref),
            (turn_hbm, turn_ref), (edge_hbm, edge_ref), (fwd_hbm, fwd_ref), (inv_hbm, inv_ref),
        ])
    ]
    for load in loads:
        load.start()

    barrier = pltpu.get_barrier_semaphore()

    def greet(k, carry):
        pl.semaphore_signal(
            barrier, inc=1, device_id={"ctx": lax.rem(me + k, blocks)}, device_id_type=MESH
        )
        return carry

    lax.fori_loop(1, blocks, greet, 0, unroll=8)
    pl.semaphore_signal(barrier, inc=1, device_id={"dp": 1 - half}, device_id_type=MESH)

    z, y, x, c = me // low, (me // (nx * nc)) % ny, (me // nc) % nx, me % nc
    heights = [((z + dz) % nz) * low for dz in range(nz)]

    def each_peer(act):
        for dz in range(1, nz):
            act(heights[dz] + me % low)

        def turn_of(r, carry):
            dy = r % ny
            dx = (r // ny) % nx
            dc = r // (ny * nx)
            place = (((y + dy) % ny) * nx + (x + dx) % nx) * nc + (c + dc) % nc
            for dz in range(nz):
                act(heights[dz] + place)
            return carry

        lax.fori_loop(1, low, turn_of, 0)

    def remote(src, dst, index, to):
        return pltpu.make_async_remote_copy(
            src_ref=src, dst_ref=dst, send_sem=send_sem.at[index], recv_sem=recv_sem.at[index],
            device_id=to, device_id_type=MESH,
        )

    def all_of(src, dst, index):
        rest = pl.ds(0, blocks - 1)
        return remote(src.at[rest], dst.at[rest], index, {"dp": 1 - half})

    def prepare(ref, send):
        for tile in range(channels // 128):
            to = slice(tile * per_tile, tile * per_tile + per_tile)
            piece = transposed(ref[:, tile * 128:(tile + 1) * 128])
            send[to] = piece.astype(BF16).reshape(per_tile, group, rows)

    loads[0].wait()
    prepare(value_ref, send_v)
    got_v[me] = send_v[me]
    loads[1].wait()
    send_f[...] = transposed(filter_ref[...]).reshape(blocks, 1, rows)
    got_f[me] = send_f[me]

    pl.semaphore_wait(barrier, blocks)

    def send_first(to):
        remote(send_v.at[to], got_v.at[me], 0, {"ctx": to}).start()
        remote(send_f.at[to], got_f.at[me], 1, {"ctx": to}).start()

    each_peer(send_first)

    loads[2].wait()
    prepare(gate_ref, send_g)
    got_g[me] = send_g[me]
    each_peer(lambda to: remote(send_g.at[to], got_g.at[me], 2, {"ctx": to}).start())

    for load in loads[3:]:
        load.wait()

    spot = lax.broadcasted_iota(jnp.int32, (blocks, blocks), 0)
    hot_old = jnp.where(old_ref[...] == spot, 1.0, 0.0).astype(BF16)
    hot_new = jnp.where(new_ref[...] == spot, 1.0, 0.0).astype(BF16)
    first_slots = lax.dot_general(
        first_ref[...], hot_old, (((1,), (1,)), ((), ())), preferred_element_type=F32
    ).astype(BF16)
    last_slots = dot(hot_new, beside(last_ref)).astype(BF16)

    column = jnp.sum(jnp.where(new_ref[...] == spot, old_ref[...], 0), axis=1, keepdims=True)
    other = lax.broadcasted_iota(jnp.int32, (blocks, blocks), 1)
    row = jnp.sum(jnp.where(spot == other, column, 0), axis=0, keepdims=True)
    route_row[...] = jnp.broadcast_to(row, route_row.shape)
    routed = pltpu.make_async_copy(route_row, route_ref, load_sem.at[len(loads)])
    routed.start()

    turn_re, turn_im = turn_ref[0], turn_ref[1]
    edge_re, edge_im = edge_ref[0:1], edge_ref[1:2]
    top = lax.broadcasted_iota(jnp.int32, (blocks, rows), 0) == 0

    def turn(part, unit):
        part = part.astype(BF16).astype(F32)
        re, im = part[:blocks], part[blocks:]
        edges[pl.ds(unit, 1), :] = im[0:1]
        im = jnp.where(top, 0.0, im)
        at = pl.ds(unit * blocks, blocks)
        turned[at, :rows] = (turn_re * re - turn_im * im).astype(BF16)
        turned[at, rows:] = (turn_re * im + turn_im * re).astype(BF16)

    edges[...] = jnp.zeros_like(edges)
    all_of(send_v, got_v, 0).wait_recv()
    wide[...] = got_v[...].astype(F32).reshape(blocks * group, rows)
    for h in range(group):
        lanes[:, h * rows:(h + 1) * rows] = wide[pl.ds(h, blocks, stride=group), :].astype(BF16)
    for h in range(0, group, 2):
        part = dot(first_slots, lanes[:, h * rows:(h + 2) * rows])
        turn(part[:, :rows], h)
        turn(part[:, rows:], h + 1)
    all_of(send_f, got_f, 1).wait_recv()
    taps = got_f[...].reshape(blocks, rows).astype(BF16)
    turn(dot(first_ref[...], taps), group)

    fwd = beside(fwd_ref)
    inv = beside(inv_ref)
    filt = dot(turned[group * blocks:(group + 1) * blocks], fwd)
    filt_re, filt_im = filt[:, :rows], filt[:, rows:]
    line = edges[...]
    edge_spec = dot(
        jnp.concatenate([(edge_re * line).astype(BF16), (edge_im * line).astype(BF16)], axis=1), fwd
    )

    def multiplied(spec, fre, fim):
        re, im = spec[:, :rows], spec[:, rows:]
        return jnp.concatenate(
            [(re * fre - im * fim).astype(BF16), (re * fim + im * fre).astype(BF16)], axis=1
        )

    edge_filt = edge_spec[group:group + 1]
    edge_inner = dot(multiplied(edge_spec, edge_filt[:, :rows], edge_filt[:, rows:]), inv)
    edges[...] = edge_re * edge_inner[:, :rows] + edge_im * edge_inner[:, rows:]

    for h in range(0, group, 2):
        spec = dot(turned[h * blocks:(h + 2) * blocks], fwd)
        prod = jnp.concatenate(
            [multiplied(spec[:blocks], filt_re, filt_im), multiplied(spec[blocks:], filt_re, filt_im)],
            axis=0,
        )
        inner = dot(prod, inv)
        for i in range(2):
            re = inner[i * blocks:(i + 1) * blocks, :rows]
            im = inner[i * blocks:(i + 1) * blocks, rows:]
            back_im = jnp.where(top, edges[h + i:h + i + 1, :], turn_re * im - turn_im * re)
            at = slice(i * rows, (i + 1) * rows)
            back[:blocks, at] = (turn_re * re + turn_im * im).astype(BF16)
            back[blocks:, at] = back_im.astype(BF16)
        mixed = dot(last_slots, back[...])
        conv[pl.ds(h, blocks, stride=group), :] = mixed[:, :rows]
        conv[pl.ds(h + 1, blocks, stride=group), :] = mixed[:, rows:]

    sublane = lax.broadcasted_iota(jnp.int32, (group, rows), 0)
    skips = jnp.zeros((group, rows), F32)
    for h in range(group):
        skips = jnp.where(sublane == h, skip_ref[me * group + h], skips)

    routed.wait()
    all_of(send_g, got_g, 2).wait_recv()

    def gate(to):
        slot = route_ref[0, to]
        tile = conv[pl.ds(pl.multiple_of(to * group, group), group), :]
        values = got_v[slot].astype(F32)
        return (got_g[slot].astype(F32) * (tile + skips * values)).astype(BF16)

    def send_out(to):
        send_o[to] = gate(to)
        remote(send_o.at[to], got_o.at[me], 3, {"ctx": to}).start()

    got_o[me] = gate(me)
    each_peer(send_out)
    all_of(send_v, got_v, 0).wait_send()
    all_of(send_f, got_f, 1).wait_send()
    all_of(send_g, got_g, 2).wait_send()
    all_of(send_o, got_o, 3).wait_recv()

    full = got_o[...].astype(F32).reshape(blocks * group, rows)
    sums[...] = jnp.broadcast_to(jnp.sum(full * full, axis=0, keepdims=True), sums.shape)
    swap = remote(sums, partner_sums, 4, {"dp": 1 - half})
    swap.start()
    for tile in range(channels // 128):
        piece = got_o[tile * per_tile:(tile + 1) * per_tile].reshape(128, rows)
        out_ref[:, tile * 128:(tile + 1) * 128] = transposed(piece).astype(BF16)
    store = pltpu.make_async_copy(out_ref, out_hbm, load_sem.at[len(loads) + 1])
    store.start()
    swap.wait()
    scale_ref[...] = lax.rsqrt((sums[0:1] + partner_sums[0:1]) / (2 * channels) + 1e-05)
    store.wait()
    all_of(send_o, got_o, 3).wait_send()


def body(sizes, value_rows, gate_rows, filter_rows, skip, old_owner, new_owner):
    blocks = lax.axis_size("ctx")
    rows, channels = value_rows.shape
    group = channels // blocks
    tables = [jnp.asarray(t) for t in make_tables(blocks, rows)]
    hbm = pl.BlockSpec(memory_space=pltpu.HBM)
    vmem = pl.BlockSpec(memory_space=pltpu.VMEM)
    smem = pl.BlockSpec(memory_space=pltpu.SMEM)
    slots = pltpu.VMEM((blocks, group, rows), BF16)
    lines = pltpu.VMEM((blocks, 1, rows), F32)
    owners = (old_owner.reshape(1, blocks), new_owner.reshape(1, blocks))
    arrays = (value_rows, gate_rows, filter_rows, *owners, *tables)
    loaded = [pltpu.VMEM(t.shape, t.dtype) for t in arrays]
    mixed, scale = pl.pallas_call(
        functools.partial(kernel, blocks, group, sizes),
        out_shape=[
            jax.ShapeDtypeStruct((rows, channels), BF16),
            jax.ShapeDtypeStruct((1, rows), F32),
        ],
        in_specs=[smem] + [hbm] * len(arrays),
        out_specs=[hbm, vmem],
        scratch_shapes=[pltpu.VMEM((rows, channels), BF16)] + loaded + [
            slots, slots, lines, slots, slots, lines, slots, slots,
            pltpu.VMEM((blocks * group, rows), F32),
            pltpu.VMEM((blocks, group * rows), BF16),
            pltpu.VMEM(((group + 1) * blocks, 2 * rows), BF16),
            pltpu.VMEM((2 * blocks, 2 * rows), BF16),
            pltpu.VMEM((blocks * group, rows), F32),
            pltpu.VMEM((group + 16, rows), F32),
            pltpu.VMEM((8, rows), F32),
            pltpu.VMEM((8, rows), F32),
            pltpu.VMEM((8, blocks), jnp.int32),
            pltpu.SMEM((8, blocks), jnp.int32),
            pltpu.SemaphoreType.DMA((len(arrays) + 2,)),
            pltpu.SemaphoreType.DMA((5,)),
            pltpu.SemaphoreType.DMA((5,)),
        ],
        compiler_params=pltpu.CompilerParams(
            collective_id=0, has_side_effects=True, vmem_limit_bytes=64 << 20
        ),
    )(skip, *arrays)
    return (mixed.astype(F32) * scale.reshape(rows, 1)).astype(BF16)


def solution(mesh):
    placed = (P("ctx", "dp"), P("ctx", "dp"), P("ctx", "dp"), P("dp"), P(), P())
    sizes = (8, 4, 2, 2)
    return jax.shard_map(
        functools.partial(body, sizes), mesh=mesh, in_specs=placed, out_specs=P("ctx", "dp"), check_vma=False
    )
```

```python
import functools
import math

import jax
import jax.numpy as jnp
import numpy as np
from jax import lax
from jax.experimental import pallas as pl
from jax.experimental.pallas import tpu as pltpu
from jax.sharding import PartitionSpec as P

MESH = pl.DeviceIdType.MESH
F32 = jnp.float32
BF16 = jnp.bfloat16


def twist(indices, period):
    wrapped = indices % period
    mirror = np.minimum(wrapped, period - wrapped)
    angles = mirror.astype(np.float64) * (2.0 * math.pi / period)
    sines = np.where((mirror == 0) | (2 * mirror == period), 0.0, np.sin(angles))
    sines = np.where(wrapped > period - wrapped, -sines, sines)
    return np.cos(angles), -sines


def make_tables(blocks, rows):
    period, full = 2 * blocks, 2 * blocks * rows
    a, b = np.arange(blocks), np.arange(rows)
    re, im = twist(a[:, None] * a[None, :], period)
    edge = twist(np.full((1, 1), blocks) * a[None, :], period)[0]
    im[:1] = edge
    first = np.concatenate([re, im], axis=0)
    weight = np.full((blocks, 1), 2.0 / full)
    weight[0] = 1.0 / full
    last = np.concatenate([re * weight, im * weight], axis=0)
    turn_re, turn_im = twist(a[:, None] * b[None, :], full)
    edge_re, edge_im = twist(blocks * b[None, :], full)
    dre, dim = twist(b[:, None] * b[None, :], rows)
    fwd = np.block([[dre, dim], [-dim, dre]])
    inv = np.block([[dre, -dim], [dim, dre]])
    low = lambda t: np.asarray(t, np.float32).astype(jnp.bfloat16)
    wide = lambda t: np.asarray(t, np.float32)
    return (
        low(first),
        low(np.concatenate([last[:blocks].T, last[blocks:].T], axis=0)),
        low(np.concatenate([fwd[:, :rows], fwd[:, rows:]], axis=0)),
        low(np.concatenate([inv[:, :rows], inv[:, rows:]], axis=0)),
        np.stack([wide(turn_re), wide(turn_im)]),
        np.concatenate([wide(edge_re), wide(edge_im)], axis=0),
    )


def transposed(tile):
    return tile.astype(F32).T


def beside(ref):
    depth = ref.shape[0] // 2
    return jnp.concatenate([ref[:depth], ref[depth:]], axis=1)


def dot(x, y):
    return jnp.dot(x, y, preferred_element_type=F32)


def kernel(
    blocks, group, sizes,
    skip_ref, value_hbm, gate_hbm, filter_hbm, old_hbm, new_hbm,
    first_hbm, last_hbm, fwd_hbm, inv_hbm, turn_hbm, edge_hbm,
    out_hbm, out_ref,
    value_ref, gate_ref, filter_ref, old_ref, new_ref,
    first_ref, last_ref, fwd_ref, inv_ref, turn_ref, edge_ref,
    send_v, send_g, send_f, got_v, got_g, got_f, send_o, got_o,
    wide, lanes, turned, back, conv, edges, sums, partner_sums, route_row, route_ref,
    load_sem, send_sem, recv_sem,
):
    me = lax.axis_index("ctx")
    half = lax.axis_index("dp")
    rows, channels = value_ref.shape
    per_tile = 128 // group
    nz, ny, nx, nc = sizes
    low = ny * nx * nc

    loads = [
        pltpu.make_async_copy(src, dst, load_sem.at[i])
        for i, (src, dst) in enumerate([
            (value_hbm, value_ref), (filter_hbm, filter_ref), (gate_hbm, gate_ref),
            (old_hbm, old_ref), (new_hbm, new_ref), (first_hbm, first_ref), (last_hbm, last_ref),
            (turn_hbm, turn_ref), (edge_hbm, edge_ref), (fwd_hbm, fwd_ref), (inv_hbm, inv_ref),
        ])
    ]
    for load in loads:
        load.start()

    barrier = pltpu.get_barrier_semaphore()

    def greet(k, carry):
        pl.semaphore_signal(
            barrier, inc=1, device_id={"ctx": lax.rem(me + k, blocks)}, device_id_type=MESH
        )
        return carry

    lax.fori_loop(1, blocks, greet, 0, unroll=8)
    pl.semaphore_signal(barrier, inc=1, device_id={"dp": 1 - half}, device_id_type=MESH)

    z, y, x, c = me // low, (me // (nx * nc)) % ny, (me // nc) % nx, me % nc
    heights = [((z + dz) % nz) * low for dz in range(nz)]

    def each_peer(act):
        steps = (4, 3, 5, 2, 6, 1, 7, 0)

        def turn_of(i, carry):
            r = low - 1 - i
            dy = r % ny
            dx = (r // ny) % nx
            dc = r // (ny * nx)
            place = (((y + dy) % ny) * nx + (x + dx) % nx) * nc + (c + dc) % nc
            for dz in steps:
                act(heights[dz] + place)
            return carry

        lax.fori_loop(0, low - 1, turn_of, 0)
        for dz in steps[:-1]:
            act(heights[dz] + me % low)

    def remote(src, dst, index, to):
        return pltpu.make_async_remote_copy(
            src_ref=src, dst_ref=dst, send_sem=send_sem.at[index], recv_sem=recv_sem.at[index],
            device_id=to, device_id_type=MESH,
        )

    def all_of(src, dst, index):
        rest = pl.ds(0, blocks - 1)
        return remote(src.at[rest], dst.at[rest], index, {"dp": 1 - half})

    def prepare(ref, send):
        for tile in range(channels // 128):
            to = slice(tile * per_tile, tile * per_tile + per_tile)
            piece = transposed(ref[:, tile * 128:(tile + 1) * 128])
            send[to] = piece.astype(BF16).reshape(per_tile, group, rows)

    loads[0].wait()
    prepare(value_ref, send_v)
    got_v[me] = send_v[me]
    loads[1].wait()
    send_f[...] = transposed(filter_ref[...]).reshape(blocks, 1, rows)
    got_f[me] = send_f[me]

    pl.semaphore_wait(barrier, blocks)

    def send_first(to):
        remote(send_v.at[to], got_v.at[me], 0, {"ctx": to}).start()
        remote(send_f.at[to], got_f.at[me], 1, {"ctx": to}).start()

    each_peer(send_first)

    loads[2].wait()
    prepare(gate_ref, send_g)
    got_g[me] = send_g[me]
    each_peer(lambda to: remote(send_g.at[to], got_g.at[me], 2, {"ctx": to}).start())

    for load in loads[3:]:
        load.wait()

    spot = lax.broadcasted_iota(jnp.int32, (blocks, blocks), 0)
    hot_old = jnp.where(old_ref[...] == spot, 1.0, 0.0).astype(BF16)
    hot_new = jnp.where(new_ref[...] == spot, 1.0, 0.0).astype(BF16)
    first_slots = lax.dot_general(
        first_ref[...], hot_old, (((1,), (1,)), ((), ())), preferred_element_type=F32
    ).astype(BF16)
    last_slots = dot(hot_new, beside(last_ref)).astype(BF16)

    column = jnp.sum(jnp.where(new_ref[...] == spot, old_ref[...], 0), axis=1, keepdims=True)
    other = lax.broadcasted_iota(jnp.int32, (blocks, blocks), 1)
    row = jnp.sum(jnp.where(spot == other, column, 0), axis=0, keepdims=True)
    route_row[...] = jnp.broadcast_to(row, route_row.shape)
    routed = pltpu.make_async_copy(route_row, route_ref, load_sem.at[len(loads)])
    routed.start()

    turn_re, turn_im = turn_ref[0], turn_ref[1]
    edge_re, edge_im = edge_ref[0:1], edge_ref[1:2]
    top = lax.broadcasted_iota(jnp.int32, (blocks, rows), 0) == 0

    def turn(part, unit):
        part = part.astype(BF16).astype(F32)
        re, im = part[:blocks], part[blocks:]
        edges[pl.ds(unit, 1), :] = im[0:1]
        im = jnp.where(top, 0.0, im)
        at = pl.ds(unit * blocks, blocks)
        turned[at, :rows] = (turn_re * re - turn_im * im).astype(BF16)
        turned[at, rows:] = (turn_re * im + turn_im * re).astype(BF16)

    edges[...] = jnp.zeros_like(edges)
    all_of(send_v, got_v, 0).wait_recv()
    wide[...] = got_v[...].astype(F32).reshape(blocks * group, rows)
    for h in range(group):
        lanes[:, h * rows:(h + 1) * rows] = wide[pl.ds(h, blocks, stride=group), :].astype(BF16)
    for h in range(0, group, 2):
        part = dot(first_slots, lanes[:, h * rows:(h + 2) * rows])
        turn(part[:, :rows], h)
        turn(part[:, rows:], h + 1)
    all_of(send_f, got_f, 1).wait_recv()
    taps = got_f[...].reshape(blocks, rows).astype(BF16)
    turn(dot(first_ref[...], taps), group)

    fwd = beside(fwd_ref)
    inv = beside(inv_ref)
    filt = dot(turned[group * blocks:(group + 1) * blocks], fwd)
    filt_re, filt_im = filt[:, :rows], filt[:, rows:]
    line = edges[...]
    edge_spec = dot(
        jnp.concatenate([(edge_re * line).astype(BF16), (edge_im * line).astype(BF16)], axis=1), fwd
    )

    def multiplied(spec, fre, fim):
        re, im = spec[:, :rows], spec[:, rows:]
        return jnp.concatenate(
            [(re * fre - im * fim).astype(BF16), (re * fim + im * fre).astype(BF16)], axis=1
        )

    edge_filt = edge_spec[group:group + 1]
    edge_inner = dot(multiplied(edge_spec, edge_filt[:, :rows], edge_filt[:, rows:]), inv)
    edges[...] = edge_re * edge_inner[:, :rows] + edge_im * edge_inner[:, rows:]

    for h in range(0, group, 2):
        spec = dot(turned[h * blocks:(h + 2) * blocks], fwd)
        prod = jnp.concatenate(
            [multiplied(spec[:blocks], filt_re, filt_im), multiplied(spec[blocks:], filt_re, filt_im)],
            axis=0,
        )
        inner = dot(prod, inv)
        for i in range(2):
            re = inner[i * blocks:(i + 1) * blocks, :rows]
            im = inner[i * blocks:(i + 1) * blocks, rows:]
            back_im = jnp.where(top, edges[h + i:h + i + 1, :], turn_re * im - turn_im * re)
            at = slice(i * rows, (i + 1) * rows)
            back[:blocks, at] = (turn_re * re + turn_im * im).astype(BF16)
            back[blocks:, at] = back_im.astype(BF16)
        mixed = dot(last_slots, back[...])
        conv[pl.ds(h, blocks, stride=group), :] = mixed[:, :rows]
        conv[pl.ds(h + 1, blocks, stride=group), :] = mixed[:, rows:]

    sublane = lax.broadcasted_iota(jnp.int32, (group, rows), 0)
    skips = jnp.zeros((group, rows), F32)
    for h in range(group):
        skips = jnp.where(sublane == h, skip_ref[me * group + h], skips)

    routed.wait()
    all_of(send_g, got_g, 2).wait_recv()

    def gate(to):
        slot = route_ref[0, to]
        tile = conv[pl.ds(pl.multiple_of(to * group, group), group), :]
        values = got_v[slot].astype(F32)
        return (got_g[slot].astype(F32) * (tile + skips * values)).astype(BF16)

    def send_out(to):
        send_o[to] = gate(to)
        remote(send_o.at[to], got_o.at[me], 3, {"ctx": to}).start()

    got_o[me] = gate(me)
    each_peer(send_out)
    all_of(send_v, got_v, 0).wait_send()
    all_of(send_f, got_f, 1).wait_send()
    all_of(send_g, got_g, 2).wait_send()
    all_of(send_o, got_o, 3).wait_recv()

    full = got_o[...].astype(F32).reshape(blocks * group, rows)
    sums[...] = jnp.broadcast_to(jnp.sum(full * full, axis=0, keepdims=True), sums.shape)
    swap = remote(sums, partner_sums, 4, {"dp": 1 - half})
    swap.start()
    for tile in range(channels // 128):
        piece = got_o[tile * per_tile:(tile + 1) * per_tile].reshape(128, rows)
        out_ref[:, tile * 128:(tile + 1) * 128] = transposed(piece).astype(BF16)
    swap.wait()
    scale = lax.rsqrt((sums[...] + partner_sums[...]) / (2 * channels) + 1e-05).T[:, 0:1]
    stores = []
    for i in range(4):
        at = slice(i * (channels // 4), (i + 1) * (channels // 4))
        out_ref[:, at] = (out_ref[:, at].astype(F32) * scale).astype(BF16)
        stores.append(
            pltpu.make_async_copy(out_ref.at[:, at], out_hbm.at[:, at], load_sem.at[len(loads) + 1 + i])
        )
        stores[-1].start()
    for store in stores:
        store.wait()
    all_of(send_o, got_o, 3).wait_send()


def body(sizes, value_rows, gate_rows, filter_rows, skip, old_owner, new_owner):
    blocks = lax.axis_size("ctx")
    rows, channels = value_rows.shape
    group = channels // blocks
    tables = [jnp.asarray(t) for t in make_tables(blocks, rows)]
    hbm = pl.BlockSpec(memory_space=pltpu.HBM)
    smem = pl.BlockSpec(memory_space=pltpu.SMEM)
    slots = pltpu.VMEM((blocks, group, rows), BF16)
    lines = pltpu.VMEM((blocks, 1, rows), F32)
    owners = (old_owner.reshape(1, blocks), new_owner.reshape(1, blocks))
    arrays = (value_rows, gate_rows, filter_rows, *owners, *tables)
    loaded = [pltpu.VMEM(t.shape, t.dtype) for t in arrays]
    return pl.pallas_call(
        functools.partial(kernel, blocks, group, sizes),
        out_shape=jax.ShapeDtypeStruct((rows, channels), BF16),
        in_specs=[smem] + [hbm] * len(arrays),
        out_specs=hbm,
        scratch_shapes=[pltpu.VMEM((rows, channels), BF16)] + loaded + [
            slots, slots, lines, slots, slots, lines, slots, slots,
            pltpu.VMEM((blocks * group, rows), F32),
            pltpu.VMEM((blocks, group * rows), BF16),
            pltpu.VMEM(((group + 1) * blocks, 2 * rows), BF16),
            pltpu.VMEM((2 * blocks, 2 * rows), BF16),
            pltpu.VMEM((blocks * group, rows), F32),
            pltpu.VMEM((group + 16, rows), F32),
            pltpu.VMEM((8, rows), F32),
            pltpu.VMEM((8, rows), F32),
            pltpu.VMEM((8, blocks), jnp.int32),
            pltpu.SMEM((8, blocks), jnp.int32),
            pltpu.SemaphoreType.DMA((len(arrays) + 5,)),
            pltpu.SemaphoreType.DMA((5,)),
            pltpu.SemaphoreType.DMA((5,)),
        ],
        compiler_params=pltpu.CompilerParams(
            collective_id=0, has_side_effects=True, vmem_limit_bytes=64 << 20
        ),
    )(skip, *arrays)


def solution(mesh):
    placed = (P("ctx", "dp"), P("ctx", "dp"), P("ctx", "dp"), P("dp"), P(), P())
    sizes = (8, 4, 2, 2)
    return jax.shard_map(
        functools.partial(body, sizes), mesh=mesh, in_specs=placed, out_specs=P("ctx", "dp"), check_vma=False
    )
```

```python
import functools
import math

import jax
import jax.numpy as jnp
import numpy as np
from jax import lax
from jax.experimental import pallas as pl
from jax.experimental.pallas import tpu as pltpu
from jax.sharding import PartitionSpec as P

MESH = pl.DeviceIdType.MESH
F32 = jnp.float32
BF16 = jnp.bfloat16


def twist(indices, period):
    wrapped = indices % period
    mirror = np.minimum(wrapped, period - wrapped)
    angles = mirror.astype(np.float64) * (2.0 * math.pi / period)
    sines = np.where((mirror == 0) | (2 * mirror == period), 0.0, np.sin(angles))
    sines = np.where(wrapped > period - wrapped, -sines, sines)
    return np.cos(angles), -sines


def make_tables(blocks, rows):
    period, full = 2 * blocks, 2 * blocks * rows
    a, b = np.arange(blocks), np.arange(rows)
    re, im = twist(a[:, None] * a[None, :], period)
    edge = twist(np.full((1, 1), blocks) * a[None, :], period)[0]
    im[:1] = edge
    first = np.concatenate([re, im], axis=0)
    weight = np.full((blocks, 1), 2.0 / full)
    weight[0] = 1.0 / full
    last = np.concatenate([re * weight, im * weight], axis=0)
    turn_re, turn_im = twist(a[:, None] * b[None, :], full)
    edge_re, edge_im = twist(blocks * b[None, :], full)
    dre, dim = twist(b[:, None] * b[None, :], rows)
    fwd = np.block([[dre, dim], [-dim, dre]])
    inv = np.block([[dre, -dim], [dim, dre]])
    low = lambda t: np.asarray(t, np.float32).astype(jnp.bfloat16)
    wide = lambda t: np.asarray(t, np.float32)
    return (
        low(first),
        low(np.concatenate([last[:blocks].T, last[blocks:].T], axis=0)),
        low(np.concatenate([fwd[:, :rows], fwd[:, rows:]], axis=0)),
        low(np.concatenate([inv[:, :rows], inv[:, rows:]], axis=0)),
        np.stack([wide(turn_re), wide(turn_im)]),
        np.concatenate([wide(edge_re), wide(edge_im)], axis=0),
    )


def transposed(tile):
    return tile.astype(F32).T


def beside(ref):
    depth = ref.shape[0] // 2
    return jnp.concatenate([ref[:depth], ref[depth:]], axis=1)


def dot(x, y):
    return jnp.dot(x, y, preferred_element_type=F32)


def kernel(
    blocks, group, sizes,
    skip_ref, value_hbm, gate_hbm, filter_hbm, old_hbm, new_hbm,
    first_hbm, last_hbm, fwd_hbm, inv_hbm, turn_hbm, edge_hbm,
    out_hbm, out_ref,
    value_ref, gate_ref, filter_ref, old_ref, new_ref,
    first_ref, last_ref, fwd_ref, inv_ref, turn_ref, edge_ref,
    send_v, send_g, got_v, got_g, send_o, got_o, send_f, got_f, send_f2, got_f2,
    wide, lanes, turned, back, conv, edges, sums, partner_sums, route_row, route_ref,
    load_sem, send_sem, recv_sem,
):
    me = lax.axis_index("ctx")
    half = lax.axis_index("dp")
    rows, channels = value_ref.shape
    per_tile = 128 // group
    nz, ny, nx, nc = sizes
    low = ny * nx * nc

    loads = [
        pltpu.make_async_copy(src, dst, load_sem.at[i])
        for i, (src, dst) in enumerate([
            (value_hbm, value_ref), (filter_hbm, filter_ref), (gate_hbm, gate_ref),
            (old_hbm, old_ref), (new_hbm, new_ref), (first_hbm, first_ref), (last_hbm, last_ref),
            (turn_hbm, turn_ref), (edge_hbm, edge_ref), (fwd_hbm, fwd_ref), (inv_hbm, inv_ref),
        ])
    ]
    for load in loads:
        load.start()

    barrier = pltpu.get_barrier_semaphore()

    def greet(k, carry):
        pl.semaphore_signal(
            barrier, inc=1, device_id={"ctx": lax.rem(me + k, blocks)}, device_id_type=MESH
        )
        return carry

    lax.fori_loop(1, blocks, greet, 0, unroll=8)
    pl.semaphore_signal(barrier, inc=1, device_id={"dp": 1 - half}, device_id_type=MESH)

    z, y, x, c = me // low, (me // (nx * nc)) % ny, (me // nc) % nx, me % nc
    heights = [((z + dz) % nz) * low for dz in range(nz)]

    def each_peer(act):
        steps = (4, 3, 5, 2, 6, 1, 7, 0)

        def turn_of(i, carry):
            r = low - 1 - i
            dy = r % ny
            dx = (r // ny) % nx
            dc = r // (ny * nx)
            place = (((y + dy) % ny) * nx + (x + dx) % nx) * nc + (c + dc) % nc
            for dz in steps:
                act(heights[dz] + place)
            return carry

        lax.fori_loop(0, low - 1, turn_of, 0)
        for dz in steps[:-1]:
            act(heights[dz] + me % low)

    def remote(src, dst, index, to):
        return pltpu.make_async_remote_copy(
            src_ref=src, dst_ref=dst, send_sem=send_sem.at[index], recv_sem=recv_sem.at[index],
            device_id=to, device_id_type=MESH,
        )

    def all_of(src, dst, index):
        rest = pl.ds(0, blocks - 1)
        return remote(src.at[rest], dst.at[rest], index, {"dp": 1 - half})

    def prepare(ref, send):
        for tile in range(channels // 128):
            to = slice(tile * per_tile, tile * per_tile + per_tile)
            piece = transposed(ref[:, tile * 128:(tile + 1) * 128])
            send[to] = piece.astype(BF16).reshape(per_tile, group, rows)

    loads[0].wait()
    prepare(value_ref, send_v)
    got_v[me] = send_v[me]
    loads[1].wait()
    here = me % low
    wide[:blocks] = transposed(filter_ref[...])
    for place in range(low):
        send_f[place * nz:(place + 1) * nz] = wide[pl.ds(place, nz, stride=low), :]

    def of_place(ref, place):
        return ref.at[pl.ds(pl.multiple_of(place * nz, nz), nz)]

    own = pl.ds(pl.multiple_of(here * nz, nz), nz)
    got_f[own, :] = send_f[own, :]

    pl.semaphore_wait(barrier, blocks)

    for step in range(1, low):
        place = (here + step) % low
        remote(of_place(send_f, place), of_place(got_f, here), 1, {"ctx": z * low + place}).start()
    each_peer(lambda to: remote(send_v.at[to], got_v.at[me], 0, {"ctx": to}).start())

    loads[2].wait()
    prepare(gate_ref, send_g)
    got_g[me] = send_g[me]
    rest = pl.ds(0, (low - 1) * nz)
    first_hop = remote(send_f.at[rest], got_f.at[rest], 1, {"dp": 1 - half})
    first_hop.wait_recv()
    for height in range(nz):
        send_f2[height] = got_f[pl.ds(height, low, stride=nz), :].astype(BF16)
    got_f2[z] = send_f2[z]
    for dz in range(1, nz):
        height = (z + dz) % nz
        remote(send_f2.at[height], got_f2.at[z], 5, {"ctx": height * low + here}).start()
    rest = pl.ds(0, nz - 1)
    second_hop = remote(send_f2.at[rest], got_f2.at[rest], 5, {"dp": 1 - half})
    each_peer(lambda to: remote(send_g.at[to], got_g.at[me], 2, {"ctx": to}).start())

    for load in loads[3:]:
        load.wait()

    spot = lax.broadcasted_iota(jnp.int32, (blocks, blocks), 0)
    hot_old = jnp.where(old_ref[...] == spot, 1.0, 0.0).astype(BF16)
    hot_new = jnp.where(new_ref[...] == spot, 1.0, 0.0).astype(BF16)
    first_slots = lax.dot_general(
        first_ref[...], hot_old, (((1,), (1,)), ((), ())), preferred_element_type=F32
    ).astype(BF16)
    last_slots = dot(hot_new, beside(last_ref)).astype(BF16)

    column = jnp.sum(jnp.where(new_ref[...] == spot, old_ref[...], 0), axis=1, keepdims=True)
    other = lax.broadcasted_iota(jnp.int32, (blocks, blocks), 1)
    row = jnp.sum(jnp.where(spot == other, column, 0), axis=0, keepdims=True)
    route_row[...] = jnp.broadcast_to(row, route_row.shape)
    routed = pltpu.make_async_copy(route_row, route_ref, load_sem.at[len(loads)])
    routed.start()

    turn_re, turn_im = turn_ref[0], turn_ref[1]
    edge_re, edge_im = edge_ref[0:1], edge_ref[1:2]
    top = lax.broadcasted_iota(jnp.int32, (blocks, rows), 0) == 0

    def turn(part, unit):
        part = part.astype(BF16).astype(F32)
        re, im = part[:blocks], part[blocks:]
        edges[pl.ds(unit, 1), :] = im[0:1]
        im = jnp.where(top, 0.0, im)
        at = pl.ds(unit * blocks, blocks)
        turned[at, :rows] = (turn_re * re - turn_im * im).astype(BF16)
        turned[at, rows:] = (turn_re * im + turn_im * re).astype(BF16)

    edges[...] = jnp.zeros_like(edges)
    all_of(send_v, got_v, 0).wait_recv()
    wide[...] = got_v[...].astype(F32).reshape(blocks * group, rows)
    for h in range(group):
        lanes[:, h * rows:(h + 1) * rows] = wide[pl.ds(h, blocks, stride=group), :].astype(BF16)
    for h in range(0, group, 2):
        part = dot(first_slots, lanes[:, h * rows:(h + 2) * rows])
        turn(part[:, :rows], h)
        turn(part[:, rows:], h + 1)
    second_hop.wait_recv()
    taps = got_f2[...].reshape(blocks, rows)
    turn(dot(first_ref[...], taps), group)

    fwd = beside(fwd_ref)
    inv = beside(inv_ref)
    filt = dot(turned[group * blocks:(group + 1) * blocks], fwd)
    filt_re, filt_im = filt[:, :rows], filt[:, rows:]
    line = edges[...]
    edge_spec = dot(
        jnp.concatenate([(edge_re * line).astype(BF16), (edge_im * line).astype(BF16)], axis=1), fwd
    )

    def multiplied(spec, fre, fim):
        re, im = spec[:, :rows], spec[:, rows:]
        return jnp.concatenate(
            [(re * fre - im * fim).astype(BF16), (re * fim + im * fre).astype(BF16)], axis=1
        )

    edge_filt = edge_spec[group:group + 1]
    edge_inner = dot(multiplied(edge_spec, edge_filt[:, :rows], edge_filt[:, rows:]), inv)
    edges[...] = edge_re * edge_inner[:, :rows] + edge_im * edge_inner[:, rows:]

    for h in range(0, group, 2):
        spec = dot(turned[h * blocks:(h + 2) * blocks], fwd)
        prod = jnp.concatenate(
            [multiplied(spec[:blocks], filt_re, filt_im), multiplied(spec[blocks:], filt_re, filt_im)],
            axis=0,
        )
        inner = dot(prod, inv)
        for i in range(2):
            re = inner[i * blocks:(i + 1) * blocks, :rows]
            im = inner[i * blocks:(i + 1) * blocks, rows:]
            back_im = jnp.where(top, edges[h + i:h + i + 1, :], turn_re * im - turn_im * re)
            at = slice(i * rows, (i + 1) * rows)
            back[:blocks, at] = (turn_re * re + turn_im * im).astype(BF16)
            back[blocks:, at] = back_im.astype(BF16)
        mixed = dot(last_slots, back[...])
        conv[pl.ds(h, blocks, stride=group), :] = mixed[:, :rows]
        conv[pl.ds(h + 1, blocks, stride=group), :] = mixed[:, rows:]

    sublane = lax.broadcasted_iota(jnp.int32, (group, rows), 0)
    skips = jnp.zeros((group, rows), F32)
    for h in range(group):
        skips = jnp.where(sublane == h, skip_ref[me * group + h], skips)

    routed.wait()
    all_of(send_g, got_g, 2).wait_recv()

    def gate(to):
        slot = route_ref[0, to]
        tile = conv[pl.ds(pl.multiple_of(to * group, group), group), :]
        values = got_v[slot].astype(F32)
        return (got_g[slot].astype(F32) * (tile + skips * values)).astype(BF16)

    def send_out(to):
        send_o[to] = gate(to)
        remote(send_o.at[to], got_o.at[me], 3, {"ctx": to}).start()

    got_o[me] = gate(me)
    each_peer(send_out)
    all_of(send_o, got_o, 3).wait_recv()

    full = got_o[...].astype(F32).reshape(blocks * group, rows)
    sums[...] = jnp.broadcast_to(jnp.sum(full * full, axis=0, keepdims=True), sums.shape)
    swap = remote(sums, partner_sums, 4, {"dp": 1 - half})
    swap.start()
    for tile in range(channels // 128):
        piece = got_o[tile * per_tile:(tile + 1) * per_tile].reshape(128, rows)
        out_ref[:, tile * 128:(tile + 1) * 128] = transposed(piece).astype(BF16)
    swap.wait()
    scale = lax.rsqrt((sums[...] + partner_sums[...]) / (2 * channels) + 1e-05).T[:, 0:1]
    stores = []
    for i in range(4):
        at = slice(i * (channels // 4), (i + 1) * (channels // 4))
        out_ref[:, at] = (out_ref[:, at].astype(F32) * scale).astype(BF16)
        stores.append(
            pltpu.make_async_copy(out_ref.at[:, at], out_hbm.at[:, at], load_sem.at[len(loads) + 1 + i])
        )
        stores[-1].start()
    for store in stores:
        store.wait()
    all_of(send_v, got_v, 0).wait_send()
    first_hop.wait_send()
    second_hop.wait_send()
    all_of(send_g, got_g, 2).wait_send()
    all_of(send_o, got_o, 3).wait_send()


def body(sizes, value_rows, gate_rows, filter_rows, skip, old_owner, new_owner):
    blocks = lax.axis_size("ctx")
    rows, channels = value_rows.shape
    group = channels // blocks
    tables = [jnp.asarray(t) for t in make_tables(blocks, rows)]
    hbm = pl.BlockSpec(memory_space=pltpu.HBM)
    smem = pl.BlockSpec(memory_space=pltpu.SMEM)
    slots = pltpu.VMEM((blocks, group, rows), BF16)
    lines = pltpu.VMEM((blocks, rows), F32)
    ring = pltpu.VMEM((sizes[0], blocks // sizes[0], rows), BF16)
    owners = (old_owner.reshape(1, blocks), new_owner.reshape(1, blocks))
    arrays = (value_rows, gate_rows, filter_rows, *owners, *tables)
    loaded = [pltpu.VMEM(t.shape, t.dtype) for t in arrays]
    return pl.pallas_call(
        functools.partial(kernel, blocks, group, sizes),
        out_shape=jax.ShapeDtypeStruct((rows, channels), BF16),
        in_specs=[smem] + [hbm] * len(arrays),
        out_specs=hbm,
        scratch_shapes=[pltpu.VMEM((rows, channels), BF16)] + loaded + [
            slots, slots, slots, slots, slots, slots, lines, lines, ring, ring,
            pltpu.VMEM((blocks * group, rows), F32),
            pltpu.VMEM((blocks, group * rows), BF16),
            pltpu.VMEM(((group + 1) * blocks, 2 * rows), BF16),
            pltpu.VMEM((2 * blocks, 2 * rows), BF16),
            pltpu.VMEM((blocks * group, rows), F32),
            pltpu.VMEM((group + 16, rows), F32),
            pltpu.VMEM((8, rows), F32),
            pltpu.VMEM((8, rows), F32),
            pltpu.VMEM((8, blocks), jnp.int32),
            pltpu.SMEM((8, blocks), jnp.int32),
            pltpu.SemaphoreType.DMA((len(arrays) + 5,)),
            pltpu.SemaphoreType.DMA((6,)),
            pltpu.SemaphoreType.DMA((6,)),
        ],
        compiler_params=pltpu.CompilerParams(
            collective_id=0, has_side_effects=True, vmem_limit_bytes=64 << 20
        ),
    )(skip, *arrays)


def solution(mesh):
    placed = (P("ctx", "dp"), P("ctx", "dp"), P("ctx", "dp"), P("dp"), P(), P())
    sizes = (8, 4, 2, 2)
    return jax.shard_map(
        functools.partial(body, sizes), mesh=mesh, in_specs=placed, out_specs=P("ctx", "dp"), check_vma=False
    )
```

```python
import functools
import math

import jax
import jax.numpy as jnp
import numpy as np
from jax import lax
from jax.experimental import pallas as pl
from jax.experimental.pallas import tpu as pltpu
from jax.sharding import PartitionSpec as P

MESH = pl.DeviceIdType.MESH
F32 = jnp.float32
BF16 = jnp.bfloat16
PARTS = 4


def twist(indices, period):
    wrapped = indices % period
    mirror = np.minimum(wrapped, period - wrapped)
    angles = mirror.astype(np.float64) * (2.0 * math.pi / period)
    sines = np.where((mirror == 0) | (2 * mirror == period), 0.0, np.sin(angles))
    sines = np.where(wrapped > period - wrapped, -sines, sines)
    return np.cos(angles), -sines


def make_tables(blocks, rows):
    period, full = 2 * blocks, 2 * blocks * rows
    a, b = np.arange(blocks), np.arange(rows)
    re, im = twist(a[:, None] * a[None, :], period)
    edge = twist(np.full((1, 1), blocks) * a[None, :], period)[0]
    im[:1] = edge
    first = np.concatenate([re, im], axis=0)
    weight = np.full((blocks, 1), 2.0 / full)
    weight[0] = 1.0 / full
    last = np.concatenate([re * weight, im * weight], axis=0)
    turn_re, turn_im = twist(a[:, None] * b[None, :], full)
    edge_re, edge_im = twist(blocks * b[None, :], full)
    dre, dim = twist(b[:, None] * b[None, :], rows)
    fwd = np.block([[dre, dim], [-dim, dre]])
    inv = np.block([[dre, -dim], [dim, dre]])
    low = lambda t: np.asarray(t, np.float32).astype(jnp.bfloat16)
    wide = lambda t: np.asarray(t, np.float32)
    return (
        low(first),
        low(np.concatenate([last[:blocks].T, last[blocks:].T], axis=0)),
        low(np.concatenate([fwd[:, :rows], fwd[:, rows:]], axis=0)),
        low(np.concatenate([inv[:, :rows], inv[:, rows:]], axis=0)),
        np.stack([wide(turn_re), wide(turn_im)]),
        np.concatenate([wide(edge_re), wide(edge_im)], axis=0),
    )


def transposed(tile):
    return tile.astype(F32).T


def beside(ref):
    depth = ref.shape[0] // 2
    return jnp.concatenate([ref[:depth], ref[depth:]], axis=1)


def dot(x, y):
    return jnp.dot(x, y, preferred_element_type=F32)


def kernel(
    blocks, group, sizes,
    skip_ref, value_hbm, gate_hbm, filter_hbm, old_hbm, new_hbm,
    first_hbm, last_hbm, fwd_hbm, inv_hbm, turn_hbm, edge_hbm,
    mixed_hbm, sums_hbm, partner_hbm, out_ref,
    value_ref, gate_ref, filter_ref, old_ref, new_ref,
    first_ref, last_ref, fwd_ref, inv_ref, turn_ref, edge_ref,
    send_v, send_g, got_v, got_g, send_o, got_o, send_f, got_f, send_f2, got_f2,
    wide, lanes, turned, back, conv, edges, sums, route_row, route_ref,
    load_sem, send_sem, recv_sem,
):
    me = lax.axis_index("ctx")
    half = lax.axis_index("dp")
    rows, channels = value_ref.shape
    per_tile = 128 // group
    nz, ny, nx, nc = sizes
    low = ny * nx * nc

    loads = [
        pltpu.make_async_copy(src, dst, load_sem.at[i])
        for i, (src, dst) in enumerate([
            (value_hbm, value_ref), (filter_hbm, filter_ref), (gate_hbm, gate_ref),
            (old_hbm, old_ref), (new_hbm, new_ref), (first_hbm, first_ref), (last_hbm, last_ref),
            (turn_hbm, turn_ref), (edge_hbm, edge_ref), (fwd_hbm, fwd_ref), (inv_hbm, inv_ref),
        ])
    ]
    for load in loads:
        load.start()

    barrier = pltpu.get_barrier_semaphore()

    def greet(k, carry):
        pl.semaphore_signal(
            barrier, inc=1, device_id={"ctx": lax.rem(me + k, blocks)}, device_id_type=MESH
        )
        return carry

    lax.fori_loop(1, blocks, greet, 0, unroll=8)
    pl.semaphore_signal(barrier, inc=1, device_id={"dp": 1 - half}, device_id_type=MESH)

    z, y, x, c = me // low, (me // (nx * nc)) % ny, (me // nc) % nx, me % nc
    heights = [((z + dz) % nz) * low for dz in range(nz)]

    def each_peer(act):
        steps = (4, 3, 5, 2, 6, 1, 7, 0)

        def turn_of(i, carry):
            r = low - 1 - i
            dc = r % nc
            dy = (r // nc) % ny
            dx = r // (ny * nc)
            place = (((y + dy) % ny) * nx + (x + dx) % nx) * nc + (c + dc) % nc
            for dz in steps:
                act(heights[dz] + place)
            return carry

        lax.fori_loop(0, low - 1, turn_of, 0)
        for dz in steps[:-1]:
            act(heights[dz] + me % low)

    def remote(src, dst, index, to):
        return pltpu.make_async_remote_copy(
            src_ref=src, dst_ref=dst, send_sem=send_sem.at[index], recv_sem=recv_sem.at[index],
            device_id=to, device_id_type=MESH,
        )

    def all_of(src, dst, index):
        rest = pl.ds(0, blocks - 1)
        return remote(src.at[rest], dst.at[rest], index, {"dp": 1 - half})

    def prepare(ref, send):
        for tile in range(channels // 128):
            to = slice(tile * per_tile, tile * per_tile + per_tile)
            piece = transposed(ref[:, tile * 128:(tile + 1) * 128])
            send[to] = piece.astype(BF16).reshape(per_tile, group, rows)

    loads[0].wait()
    prepare(value_ref, send_v)
    got_v[me] = send_v[me]
    loads[1].wait()
    here = me % low
    wide[:blocks] = transposed(filter_ref[...])
    for place in range(low):
        send_f[place * nz:(place + 1) * nz] = wide[pl.ds(place, nz, stride=low), :]

    def of_place(ref, place):
        return ref.at[pl.ds(pl.multiple_of(place * nz, nz), nz)]

    own = pl.ds(pl.multiple_of(here * nz, nz), nz)
    got_f[own, :] = send_f[own, :]

    pl.semaphore_wait(barrier, blocks)

    for step in range(1, low):
        place = (here + step) % low
        remote(of_place(send_f, place), of_place(got_f, here), 1, {"ctx": z * low + place}).start()
    each_peer(lambda to: remote(send_v.at[to], got_v.at[me], 0, {"ctx": to}).start())

    loads[2].wait()
    prepare(gate_ref, send_g)
    got_g[me] = send_g[me]
    rest = pl.ds(0, (low - 1) * nz)
    first_hop = remote(send_f.at[rest], got_f.at[rest], 1, {"dp": 1 - half})
    first_hop.wait_recv()
    for height in range(nz):
        send_f2[height] = got_f[pl.ds(height, low, stride=nz), :].astype(BF16)
    got_f2[z] = send_f2[z]
    for dz in range(1, nz):
        height = (z + dz) % nz
        remote(send_f2.at[height], got_f2.at[z], 5, {"ctx": height * low + here}).start()
    rest = pl.ds(0, nz - 1)
    second_hop = remote(send_f2.at[rest], got_f2.at[rest], 5, {"dp": 1 - half})
    each_peer(lambda to: remote(send_g.at[to], got_g.at[me], 2, {"ctx": to}).start())

    for load in loads[3:]:
        load.wait()

    spot = lax.broadcasted_iota(jnp.int32, (blocks, blocks), 0)
    hot_old = jnp.where(old_ref[...] == spot, 1.0, 0.0).astype(BF16)
    hot_new = jnp.where(new_ref[...] == spot, 1.0, 0.0).astype(BF16)
    first_slots = lax.dot_general(
        first_ref[...], hot_old, (((1,), (1,)), ((), ())), preferred_element_type=F32
    ).astype(BF16)
    last_slots = dot(hot_new, beside(last_ref)).astype(BF16)

    column = jnp.sum(jnp.where(new_ref[...] == spot, old_ref[...], 0), axis=1, keepdims=True)
    other = lax.broadcasted_iota(jnp.int32, (blocks, blocks), 1)
    row = jnp.sum(jnp.where(spot == other, column, 0), axis=0, keepdims=True)
    route_row[...] = jnp.broadcast_to(row, route_row.shape)
    routed = pltpu.make_async_copy(route_row, route_ref, load_sem.at[len(loads)])
    routed.start()

    turn_re, turn_im = turn_ref[0], turn_ref[1]
    edge_re, edge_im = edge_ref[0:1], edge_ref[1:2]
    top = lax.broadcasted_iota(jnp.int32, (blocks, rows), 0) == 0

    def turn(part, unit):
        part = part.astype(BF16).astype(F32)
        re, im = part[:blocks], part[blocks:]
        edges[pl.ds(unit, 1), :] = im[0:1]
        im = jnp.where(top, 0.0, im)
        at = pl.ds(unit * blocks, blocks)
        turned[at, :rows] = (turn_re * re - turn_im * im).astype(BF16)
        turned[at, rows:] = (turn_re * im + turn_im * re).astype(BF16)

    edges[...] = jnp.zeros_like(edges)
    all_of(send_v, got_v, 0).wait_recv()
    wide[...] = got_v[...].astype(F32).reshape(blocks * group, rows)
    for h in range(group):
        lanes[:, h * rows:(h + 1) * rows] = wide[pl.ds(h, blocks, stride=group), :].astype(BF16)
    for h in range(0, group, 2):
        part = dot(first_slots, lanes[:, h * rows:(h + 2) * rows])
        turn(part[:, :rows], h)
        turn(part[:, rows:], h + 1)
    second_hop.wait_recv()
    taps = got_f2[...].reshape(blocks, rows)
    turn(dot(first_ref[...], taps), group)

    fwd = beside(fwd_ref)
    inv = beside(inv_ref)
    filt = dot(turned[group * blocks:(group + 1) * blocks], fwd)
    filt_re, filt_im = filt[:, :rows], filt[:, rows:]
    line = edges[...]
    edge_spec = dot(
        jnp.concatenate([(edge_re * line).astype(BF16), (edge_im * line).astype(BF16)], axis=1), fwd
    )

    def multiplied(spec, fre, fim):
        re, im = spec[:, :rows], spec[:, rows:]
        return jnp.concatenate(
            [(re * fre - im * fim).astype(BF16), (re * fim + im * fre).astype(BF16)], axis=1
        )

    edge_filt = edge_spec[group:group + 1]
    edge_inner = dot(multiplied(edge_spec, edge_filt[:, :rows], edge_filt[:, rows:]), inv)
    edges[...] = edge_re * edge_inner[:, :rows] + edge_im * edge_inner[:, rows:]

    for h in range(0, group, 2):
        spec = dot(turned[h * blocks:(h + 2) * blocks], fwd)
        prod = jnp.concatenate(
            [multiplied(spec[:blocks], filt_re, filt_im), multiplied(spec[blocks:], filt_re, filt_im)],
            axis=0,
        )
        inner = dot(prod, inv)
        for i in range(2):
            re = inner[i * blocks:(i + 1) * blocks, :rows]
            im = inner[i * blocks:(i + 1) * blocks, rows:]
            back_im = jnp.where(top, edges[h + i:h + i + 1, :], turn_re * im - turn_im * re)
            at = slice(i * rows, (i + 1) * rows)
            back[:blocks, at] = (turn_re * re + turn_im * im).astype(BF16)
            back[blocks:, at] = back_im.astype(BF16)
        mixed = dot(last_slots, back[...])
        conv[pl.ds(h, blocks, stride=group), :] = mixed[:, :rows]
        conv[pl.ds(h + 1, blocks, stride=group), :] = mixed[:, rows:]

    sublane = lax.broadcasted_iota(jnp.int32, (group, rows), 0)
    skips = jnp.zeros((group, rows), F32)
    for h in range(group):
        skips = jnp.where(sublane == h, skip_ref[me * group + h], skips)

    routed.wait()
    all_of(send_g, got_g, 2).wait_recv()

    def gate(to):
        slot = route_ref[0, to]
        tile = conv[pl.ds(pl.multiple_of(to * group, group), group), :]
        values = got_v[slot].astype(F32)
        return (got_g[slot].astype(F32) * (tile + skips * values)).astype(BF16)

    def send_out(to):
        send_o[to] = gate(to)
        remote(send_o.at[to], got_o.at[me], 3, {"ctx": to}).start()

    got_o[me] = gate(me)
    each_peer(send_out)
    all_of(send_o, got_o, 3).wait_recv()

    full = got_o[...].astype(F32).reshape(blocks * group, rows)
    sums[...] = jnp.broadcast_to(jnp.sum(full * full, axis=0, keepdims=True), sums.shape)
    swap = remote(sums, partner_hbm, 4, {"dp": 1 - half})
    swap.start()
    keep = pltpu.make_async_copy(sums, sums_hbm, load_sem.at[len(loads) + 1])
    keep.start()
    stores = []
    for i in range(2):
        for tile in range(i * channels // 256, (i + 1) * channels // 256):
            piece = got_o[tile * per_tile:(tile + 1) * per_tile].reshape(128, rows)
            out_ref[:, tile * 128:(tile + 1) * 128] = transposed(piece).astype(BF16)
        at = slice(i * channels // 2, (i + 1) * channels // 2)
        stores.append(
            pltpu.make_async_copy(out_ref.at[:, at], mixed_hbm.at[:, at], load_sem.at[len(loads) + 2 + i])
        )
        stores[-1].start()
    keep.wait()
    for store in stores:
        store.wait()
    swap.wait()
    all_of(send_v, got_v, 0).wait_send()
    first_hop.wait_send()
    second_hop.wait_send()
    all_of(send_g, got_g, 2).wait_send()
    all_of(send_o, got_o, 3).wait_send()


def scaled(whole, sums_hbm, partner_hbm, mixed_hbm, out_hbm, sums, mixed, out, in_sem, out_sem):
    rows = mixed.shape[0]
    part = rows // PARTS
    parts = [slice(i * part, (i + 1) * part) for i in range(PARTS)]
    ways = [(sums_hbm, sums.at[0]), (partner_hbm, sums.at[1])]
    ways += [(mixed_hbm.at[at], mixed.at[at]) for at in parts]
    loads = [pltpu.make_async_copy(src, dst, in_sem.at[i]) for i, (src, dst) in enumerate(ways)]
    for load in loads:
        load.start()
    for load in loads[:2]:
        load.wait()
    scale = lax.rsqrt((sums[0] + sums[1]) / whole + 1e-05).T[:, 0:1]
    stores = []
    for i, at in enumerate(parts):
        loads[2 + i].wait()
        out[at] = (mixed[at].astype(F32) * scale[at]).astype(BF16)
        stores.append(pltpu.make_async_copy(out.at[at], out_hbm.at[at], out_sem.at[i]))
        stores[-1].start()
    for store in stores:
        store.wait()


def body(sizes, value_rows, gate_rows, filter_rows, skip, old_owner, new_owner):
    blocks = lax.axis_size("ctx")
    rows, channels = value_rows.shape
    group = channels // blocks
    tables = [jnp.asarray(t) for t in make_tables(blocks, rows)]
    hbm = pl.BlockSpec(memory_space=pltpu.HBM)
    smem = pl.BlockSpec(memory_space=pltpu.SMEM)
    slots = pltpu.VMEM((blocks, group, rows), BF16)
    lines = pltpu.VMEM((blocks, rows), F32)
    ring = pltpu.VMEM((sizes[0], blocks // sizes[0], rows), BF16)
    owners = (old_owner.reshape(1, blocks), new_owner.reshape(1, blocks))
    arrays = (value_rows, gate_rows, filter_rows, *owners, *tables)
    loaded = [pltpu.VMEM(t.shape, t.dtype) for t in arrays]
    slab = pltpu.VMEM((rows, channels), BF16)
    sums = jax.ShapeDtypeStruct((8, rows), F32)
    mixed, own_sums, partner_sums = pl.pallas_call(
        functools.partial(kernel, blocks, group, sizes),
        out_shape=[jax.ShapeDtypeStruct((rows, channels), BF16), sums, sums],
        in_specs=[smem] + [hbm] * len(arrays),
        out_specs=[hbm] * 3,
        scratch_shapes=[slab] + loaded + [
            slots, slots, slots, slots, slots, slots, lines, lines, ring, ring,
            pltpu.VMEM((blocks * group, rows), F32),
            pltpu.VMEM((blocks, group * rows), BF16),
            pltpu.VMEM(((group + 1) * blocks, 2 * rows), BF16),
            pltpu.VMEM((2 * blocks, 2 * rows), BF16),
            pltpu.VMEM((blocks * group, rows), F32),
            pltpu.VMEM((group + 16, rows), F32),
            pltpu.VMEM((8, rows), F32),
            pltpu.VMEM((8, blocks), jnp.int32),
            pltpu.SMEM((8, blocks), jnp.int32),
            pltpu.SemaphoreType.DMA((len(arrays) + 4,)),
            pltpu.SemaphoreType.DMA((6,)),
            pltpu.SemaphoreType.DMA((6,)),
        ],
        compiler_params=pltpu.CompilerParams(
            collective_id=0, has_side_effects=True, vmem_limit_bytes=64 << 20
        ),
    )(skip, *arrays)
    return pl.pallas_call(
        functools.partial(scaled, channels * lax.axis_size("dp")),
        out_shape=jax.ShapeDtypeStruct((rows, channels), BF16),
        in_specs=[hbm] * 3,
        out_specs=hbm,
        scratch_shapes=[
            pltpu.VMEM((2, 8, rows), F32), slab, slab,
            pltpu.SemaphoreType.DMA((PARTS + 2,)),
            pltpu.SemaphoreType.DMA((PARTS,)),
        ],
        compiler_params=pltpu.CompilerParams(vmem_limit_bytes=64 << 20),
    )(own_sums, partner_sums, mixed)


def solution(mesh):
    placed = (P("ctx", "dp"), P("ctx", "dp"), P("ctx", "dp"), P("dp"), P(), P())
    sizes = (8, 4, 2, 2)
    return jax.shard_map(
        functools.partial(body, sizes), mesh=mesh, in_specs=placed, out_specs=P("ctx", "dp"), check_vma=False
    )
```

```python
import functools
import math

import jax
import jax.numpy as jnp
import numpy as np
from jax import lax
from jax.experimental import pallas as pl
from jax.experimental.pallas import tpu as pltpu
from jax.sharding import PartitionSpec as P

MESH = pl.DeviceIdType.MESH
F32 = jnp.float32
BF16 = jnp.bfloat16
PARTS = 4


def twist(indices, period):
    wrapped = indices % period
    mirror = np.minimum(wrapped, period - wrapped)
    angles = mirror.astype(np.float64) * (2.0 * math.pi / period)
    sines = np.where((mirror == 0) | (2 * mirror == period), 0.0, np.sin(angles))
    sines = np.where(wrapped > period - wrapped, -sines, sines)
    return np.cos(angles), -sines


def make_tables(blocks, rows):
    period, full = 2 * blocks, 2 * blocks * rows
    a, b = np.arange(blocks), np.arange(rows)
    re, im = twist(a[:, None] * a[None, :], period)
    edge = twist(np.full((1, 1), blocks) * a[None, :], period)[0]
    im[:1] = edge
    first = np.concatenate([re, im], axis=0)
    weight = np.full((blocks, 1), 2.0 / full)
    weight[0] = 1.0 / full
    last = np.concatenate([re * weight, im * weight], axis=0)
    turn_re, turn_im = twist(a[:, None] * b[None, :], full)
    edge_re, edge_im = twist(blocks * b[None, :], full)
    dre, dim = twist(b[:, None] * b[None, :], rows)
    fwd = np.block([[dre, dim], [-dim, dre]])
    inv = np.block([[dre, -dim], [dim, dre]])
    low = lambda t: np.asarray(t, np.float32).astype(jnp.bfloat16)
    wide = lambda t: np.asarray(t, np.float32)
    return (
        low(first),
        low(np.concatenate([last[:blocks].T, last[blocks:].T], axis=0)),
        low(np.concatenate([fwd[:, :rows], fwd[:, rows:]], axis=0)),
        low(np.concatenate([inv[:, :rows], inv[:, rows:]], axis=0)),
        np.stack([wide(turn_re), wide(turn_im)]),
        np.concatenate([wide(edge_re), wide(edge_im)], axis=0),
    )


def transposed(tile):
    return tile.astype(F32).T


def beside(ref):
    depth = ref.shape[0] // 2
    return jnp.concatenate([ref[:depth], ref[depth:]], axis=1)


def dot(x, y):
    return jnp.dot(x, y, preferred_element_type=F32)


def kernel(
    blocks, group, sizes,
    skip_ref, value_hbm, gate_hbm, filter_hbm, old_hbm, new_hbm,
    first_hbm, last_hbm, fwd_hbm, inv_hbm, turn_hbm, edge_hbm,
    mixed_hbm, sums_hbm, partner_hbm, out_ref,
    value_ref, gate_ref, filter_ref, old_ref, new_ref,
    first_ref, last_ref, fwd_ref, inv_ref, turn_ref, edge_ref,
    send_v, send_g, got_v, got_g, send_o, got_o, send_f, got_f, send_f2, got_f2,
    wide, lanes, turned, back, conv, edges, sums, route_row, route_ref,
    load_sem, send_sem, recv_sem,
):
    me = lax.axis_index("ctx")
    half = lax.axis_index("dp")
    rows, channels = value_ref.shape
    per_tile = 128 // group
    nz, ny, nx, nc = sizes
    low = ny * nx * nc

    loads = [
        pltpu.make_async_copy(src, dst, load_sem.at[i])
        for i, (src, dst) in enumerate([
            (value_hbm, value_ref), (filter_hbm, filter_ref), (gate_hbm, gate_ref),
            (old_hbm, old_ref), (new_hbm, new_ref), (first_hbm, first_ref), (last_hbm, last_ref),
            (turn_hbm, turn_ref), (edge_hbm, edge_ref), (fwd_hbm, fwd_ref), (inv_hbm, inv_ref),
        ])
    ]
    for load in loads:
        load.start()

    barrier = pltpu.get_barrier_semaphore()

    def greet(k, carry):
        pl.semaphore_signal(
            barrier, inc=1, device_id={"ctx": lax.rem(me + k, blocks)}, device_id_type=MESH
        )
        return carry

    lax.fori_loop(1, blocks, greet, 0, unroll=8)
    pl.semaphore_signal(barrier, inc=1, device_id={"dp": 1 - half}, device_id_type=MESH)

    z, y, x, c = me // low, (me // (nx * nc)) % ny, (me // nc) % nx, me % nc
    heights = [((z + dz) % nz) * low for dz in range(nz)]

    def each_peer(act):
        steps = (4, 3, 5, 2, 6, 1, 7, 0)

        def turn_of(i, carry):
            r = low - 1 - i
            dc = r % nc
            dy = (r // nc) % ny
            dx = r // (ny * nc)
            place = (((y + dy) % ny) * nx + (x + dx) % nx) * nc + (c + dc) % nc
            for dz in steps:
                act(heights[dz] + place)
            return carry

        lax.fori_loop(0, low - 1, turn_of, 0)
        for dz in steps[:-1]:
            act(heights[dz] + me % low)

    def remote(src, dst, index, to):
        return pltpu.make_async_remote_copy(
            src_ref=src, dst_ref=dst, send_sem=send_sem.at[index], recv_sem=recv_sem.at[index],
            device_id=to, device_id_type=MESH,
        )

    def all_of(src, dst, index):
        rest = pl.ds(0, blocks - 1)
        return remote(src.at[rest], dst.at[rest], index, {"dp": 1 - half})

    def prepare(ref, send):
        for tile in range(channels // 128):
            to = slice(tile * per_tile, tile * per_tile + per_tile)
            piece = transposed(ref[:, tile * 128:(tile + 1) * 128])
            send[to] = piece.astype(BF16).reshape(per_tile, group, rows)

    loads[0].wait()
    prepare(value_ref, send_v)
    got_v[me] = send_v[me]
    loads[1].wait()
    here = me % low
    wide[:blocks] = transposed(filter_ref[...])
    for place in range(low):
        send_f[place * nz:(place + 1) * nz] = wide[pl.ds(place, nz, stride=low), :]

    def of_place(ref, place):
        return ref.at[pl.ds(pl.multiple_of(place * nz, nz), nz)]

    own = pl.ds(pl.multiple_of(here * nz, nz), nz)
    got_f[own, :] = send_f[own, :]

    pl.semaphore_wait(barrier, blocks)

    for step in range(1, low):
        place = (here + step) % low
        remote(of_place(send_f, place), of_place(got_f, here), 1, {"ctx": z * low + place}).start()
    each_peer(lambda to: remote(send_v.at[to], got_v.at[me], 0, {"ctx": to}).start())

    loads[2].wait()
    prepare(gate_ref, send_g)
    got_g[me] = send_g[me]
    rest = pl.ds(0, (low - 1) * nz)
    first_hop = remote(send_f.at[rest], got_f.at[rest], 1, {"dp": 1 - half})
    first_hop.wait_recv()
    for height in range(nz):
        send_f2[height] = got_f[pl.ds(height, low, stride=nz), :].astype(BF16)
    got_f2[z] = send_f2[z]
    for dz in range(1, nz):
        height = (z + dz) % nz
        remote(send_f2.at[height], got_f2.at[z], 5, {"ctx": height * low + here}).start()
    rest = pl.ds(0, nz - 1)
    second_hop = remote(send_f2.at[rest], got_f2.at[rest], 5, {"dp": 1 - half})
    each_peer(lambda to: remote(send_g.at[to], got_g.at[me], 2, {"ctx": to}).start())

    for load in loads[3:]:
        load.wait()

    spot = lax.broadcasted_iota(jnp.int32, (blocks, blocks), 0)
    hot_old = jnp.where(old_ref[...] == spot, 1.0, 0.0).astype(BF16)
    hot_new = jnp.where(new_ref[...] == spot, 1.0, 0.0).astype(BF16)
    first_slots = lax.dot_general(
        first_ref[...], hot_old, (((1,), (1,)), ((), ())), preferred_element_type=F32
    ).astype(BF16)
    last_slots = dot(hot_new, beside(last_ref)).astype(BF16)

    column = jnp.sum(jnp.where(new_ref[...] == spot, old_ref[...], 0), axis=1, keepdims=True)
    other = lax.broadcasted_iota(jnp.int32, (blocks, blocks), 1)
    row = jnp.sum(jnp.where(spot == other, column, 0), axis=0, keepdims=True)
    route_row[...] = jnp.broadcast_to(row, route_row.shape)
    routed = pltpu.make_async_copy(route_row, route_ref, load_sem.at[len(loads)])
    routed.start()

    turn_re, turn_im = turn_ref[0], turn_ref[1]
    edge_re, edge_im = edge_ref[0:1], edge_ref[1:2]
    top = lax.broadcasted_iota(jnp.int32, (blocks, rows), 0) == 0

    def turn(part, unit):
        part = part.astype(BF16).astype(F32)
        re, im = part[:blocks], part[blocks:]
        edges[pl.ds(unit, 1), :] = im[0:1]
        im = jnp.where(top, 0.0, im)
        at = pl.ds(unit * blocks, blocks)
        turned[at, :rows] = (turn_re * re - turn_im * im).astype(BF16)
        turned[at, rows:] = (turn_re * im + turn_im * re).astype(BF16)

    edges[...] = jnp.zeros_like(edges)
    all_of(send_v, got_v, 0).wait_recv()
    wide[...] = got_v[...].astype(F32).reshape(blocks * group, rows)
    for h in range(group):
        lanes[:, h * rows:(h + 1) * rows] = wide[pl.ds(h, blocks, stride=group), :].astype(BF16)
    for h in range(0, group, 2):
        part = dot(first_slots, lanes[:, h * rows:(h + 2) * rows])
        turn(part[:, :rows], h)
        turn(part[:, rows:], h + 1)
    second_hop.wait_recv()
    taps = got_f2[...].reshape(blocks, rows)
    turn(dot(first_ref[...], taps), group)

    fwd = beside(fwd_ref)
    inv = beside(inv_ref)
    filt = dot(turned[group * blocks:(group + 1) * blocks], fwd)
    filt_re, filt_im = filt[:, :rows], filt[:, rows:]
    line = edges[...]
    edge_spec = dot(
        jnp.concatenate([(edge_re * line).astype(BF16), (edge_im * line).astype(BF16)], axis=1), fwd
    )

    def multiplied(spec, fre, fim):
        re, im = spec[:, :rows], spec[:, rows:]
        return jnp.concatenate(
            [(re * fre - im * fim).astype(BF16), (re * fim + im * fre).astype(BF16)], axis=1
        )

    edge_filt = edge_spec[group:group + 1]
    edge_inner = dot(multiplied(edge_spec, edge_filt[:, :rows], edge_filt[:, rows:]), inv)
    edges[...] = edge_re * edge_inner[:, :rows] + edge_im * edge_inner[:, rows:]

    for h in range(0, group, 2):
        spec = dot(turned[h * blocks:(h + 2) * blocks], fwd)
        prod = jnp.concatenate(
            [multiplied(spec[:blocks], filt_re, filt_im), multiplied(spec[blocks:], filt_re, filt_im)],
            axis=0,
        )
        inner = dot(prod, inv)
        for i in range(2):
            re = inner[i * blocks:(i + 1) * blocks, :rows]
            im = inner[i * blocks:(i + 1) * blocks, rows:]
            back_im = jnp.where(top, edges[h + i:h + i + 1, :], turn_re * im - turn_im * re)
            at = slice(i * rows, (i + 1) * rows)
            back[:blocks, at] = (turn_re * re + turn_im * im).astype(BF16)
            back[blocks:, at] = back_im.astype(BF16)
        mixed = dot(last_slots, back[...])
        conv[pl.ds(h, blocks, stride=group), :] = mixed[:, :rows]
        conv[pl.ds(h + 1, blocks, stride=group), :] = mixed[:, rows:]

    sublane = lax.broadcasted_iota(jnp.int32, (group, rows), 0)
    skips = jnp.zeros((group, rows), F32)
    for h in range(group):
        skips = jnp.where(sublane == h, skip_ref[me * group + h], skips)

    routed.wait()
    all_of(send_g, got_g, 2).wait_recv()

    def gate(to):
        slot = route_ref[0, to]
        tile = conv[pl.ds(pl.multiple_of(to * group, group), group), :]
        values = got_v[slot].astype(F32)
        return (got_g[slot].astype(F32) * (tile + skips * values)).astype(BF16)

    def send_out(to):
        send_o[to] = gate(to)
        remote(send_o.at[to], got_o.at[me], 3, {"ctx": to}).start()

    got_o[me] = gate(me)
    each_peer(send_out)
    all_of(send_o, got_o, 3).wait_recv()

    square_sums = [jnp.zeros((8, rows), F32) for _ in range(4)]
    for slot in range(0, blocks, 2):
        pieces = got_o[slot:slot + 2].astype(F32).reshape(4, 8, rows)
        square_sums = [square_sums[i] + pieces[i] * pieces[i] for i in range(4)]
    total = square_sums[0] + square_sums[1] + (square_sums[2] + square_sums[3])
    sums[...] = jnp.broadcast_to(jnp.sum(total, axis=0, keepdims=True), sums.shape)
    swap = remote(sums, partner_hbm, 4, {"dp": 1 - half})
    swap.start()
    keep = pltpu.make_async_copy(sums, sums_hbm, load_sem.at[len(loads) + 1])
    keep.start()
    stores = []
    for i in range(2):
        for tile in range(i * channels // 256, (i + 1) * channels // 256):
            piece = got_o[tile * per_tile:(tile + 1) * per_tile].reshape(128, rows)
            out_ref[:, tile * 128:(tile + 1) * 128] = transposed(piece).astype(BF16)
        at = slice(i * channels // 2, (i + 1) * channels // 2)
        stores.append(
            pltpu.make_async_copy(out_ref.at[:, at], mixed_hbm.at[:, at], load_sem.at[len(loads) + 2 + i])
        )
        stores[-1].start()
    keep.wait()
    for store in stores:
        store.wait()
    swap.wait()
    all_of(send_v, got_v, 0).wait_send()
    first_hop.wait_send()
    second_hop.wait_send()
    all_of(send_g, got_g, 2).wait_send()
    all_of(send_o, got_o, 3).wait_send()


def scaled(whole, sums_hbm, partner_hbm, mixed_hbm, out_hbm, sums, mixed, out, in_sem, out_sem):
    rows = mixed.shape[0]
    part = rows // PARTS
    parts = [slice(i * part, (i + 1) * part) for i in range(PARTS)]
    ways = [(sums_hbm, sums.at[0]), (partner_hbm, sums.at[1])]
    ways += [(mixed_hbm.at[at], mixed.at[at]) for at in parts]
    loads = [pltpu.make_async_copy(src, dst, in_sem.at[i]) for i, (src, dst) in enumerate(ways)]
    for load in loads:
        load.start()
    for load in loads[:2]:
        load.wait()
    scale = lax.rsqrt((sums[0] + sums[1]) / whole + 1e-05).T[:, 0:1]
    stores = []
    for i, at in enumerate(parts):
        loads[2 + i].wait()
        out[at] = (mixed[at].astype(F32) * scale[at]).astype(BF16)
        stores.append(pltpu.make_async_copy(out.at[at], out_hbm.at[at], out_sem.at[i]))
        stores[-1].start()
    for store in stores:
        store.wait()


def body(sizes, value_rows, gate_rows, filter_rows, skip, old_owner, new_owner):
    blocks = lax.axis_size("ctx")
    rows, channels = value_rows.shape
    group = channels // blocks
    tables = [jnp.asarray(t) for t in make_tables(blocks, rows)]
    hbm = pl.BlockSpec(memory_space=pltpu.HBM)
    smem = pl.BlockSpec(memory_space=pltpu.SMEM)
    slots = pltpu.VMEM((blocks, group, rows), BF16)
    lines = pltpu.VMEM((blocks, rows), F32)
    ring = pltpu.VMEM((sizes[0], blocks // sizes[0], rows), BF16)
    owners = (old_owner.reshape(1, blocks), new_owner.reshape(1, blocks))
    arrays = (value_rows, gate_rows, filter_rows, *owners, *tables)
    loaded = [pltpu.VMEM(t.shape, t.dtype) for t in arrays]
    slab = pltpu.VMEM((rows, channels), BF16)
    sums = jax.ShapeDtypeStruct((8, rows), F32)
    mixed, own_sums, partner_sums = pl.pallas_call(
        functools.partial(kernel, blocks, group, sizes),
        out_shape=[jax.ShapeDtypeStruct((rows, channels), BF16), sums, sums],
        in_specs=[smem] + [hbm] * len(arrays),
        out_specs=[hbm] * 3,
        scratch_shapes=[slab] + loaded + [
            slots, slots, slots, slots, slots, slots, lines, lines, ring, ring,
            pltpu.VMEM((blocks * group, rows), F32),
            pltpu.VMEM((blocks, group * rows), BF16),
            pltpu.VMEM(((group + 1) * blocks, 2 * rows), BF16),
            pltpu.VMEM((2 * blocks, 2 * rows), BF16),
            pltpu.VMEM((blocks * group, rows), F32),
            pltpu.VMEM((group + 16, rows), F32),
            pltpu.VMEM((8, rows), F32),
            pltpu.VMEM((8, blocks), jnp.int32),
            pltpu.SMEM((8, blocks), jnp.int32),
            pltpu.SemaphoreType.DMA((len(arrays) + 4,)),
            pltpu.SemaphoreType.DMA((6,)),
            pltpu.SemaphoreType.DMA((6,)),
        ],
        compiler_params=pltpu.CompilerParams(
            collective_id=0, has_side_effects=True, vmem_limit_bytes=64 << 20
        ),
    )(skip, *arrays)
    return pl.pallas_call(
        functools.partial(scaled, channels * lax.axis_size("dp")),
        out_shape=jax.ShapeDtypeStruct((rows, channels), BF16),
        in_specs=[hbm] * 3,
        out_specs=hbm,
        scratch_shapes=[
            pltpu.VMEM((2, 8, rows), F32), slab, slab,
            pltpu.SemaphoreType.DMA((PARTS + 2,)),
            pltpu.SemaphoreType.DMA((PARTS,)),
        ],
        compiler_params=pltpu.CompilerParams(vmem_limit_bytes=64 << 20),
    )(own_sums, partner_sums, mixed)


def solution(mesh):
    placed = (P("ctx", "dp"), P("ctx", "dp"), P("ctx", "dp"), P("dp"), P(), P())
    sizes = (8, 4, 2, 2)
    return jax.shard_map(
        functools.partial(body, sizes), mesh=mesh, in_specs=placed, out_specs=P("ctx", "dp"), check_vma=False
    )
```

```python
import functools
import math

import jax
import jax.numpy as jnp
import numpy as np
from jax import lax
from jax.experimental import pallas as pl
from jax.experimental.pallas import tpu as pltpu
from jax.sharding import PartitionSpec as P

MESH = pl.DeviceIdType.MESH
F32 = jnp.float32
BF16 = jnp.bfloat16
PARTS = 4


def twist(indices, period):
    wrapped = indices % period
    mirror = np.minimum(wrapped, period - wrapped)
    angles = mirror.astype(np.float64) * (2.0 * math.pi / period)
    sines = np.where((mirror == 0) | (2 * mirror == period), 0.0, np.sin(angles))
    sines = np.where(wrapped > period - wrapped, -sines, sines)
    return np.cos(angles), -sines


def make_tables(blocks, rows):
    period, full = 2 * blocks, 2 * blocks * rows
    a, b = np.arange(blocks), np.arange(rows)
    re, im = twist(a[:, None] * a[None, :], period)
    edge = twist(np.full((1, 1), blocks) * a[None, :], period)[0]
    im[:1] = edge
    first = np.concatenate([re, im], axis=0)
    weight = np.full((blocks, 1), 2.0 / full)
    weight[0] = 1.0 / full
    last = np.concatenate([re * weight, im * weight], axis=0)
    turn_re, turn_im = twist(a[:, None] * b[None, :], full)
    edge_re, edge_im = twist(blocks * b[None, :], full)
    dre, dim = twist(b[:, None] * b[None, :], rows)
    fwd = np.block([[dre, dim], [-dim, dre]])
    inv = np.block([[dre, -dim], [dim, dre]])
    low = lambda t: np.asarray(t, np.float32).astype(jnp.bfloat16)
    wide = lambda t: np.asarray(t, np.float32)
    return (
        low(first),
        low(np.concatenate([last[:blocks].T, last[blocks:].T], axis=0)),
        low(np.concatenate([fwd[:, :rows], fwd[:, rows:]], axis=0)),
        low(np.concatenate([inv[:, :rows], inv[:, rows:]], axis=0)),
        np.stack([wide(turn_re), wide(turn_im)]),
        np.concatenate([wide(edge_re), wide(edge_im)], axis=0),
    )


def transposed(tile):
    return tile.astype(F32).T


def beside(ref):
    depth = ref.shape[0] // 2
    return jnp.concatenate([ref[:depth], ref[depth:]], axis=1)


def dot(x, y):
    return jnp.dot(x, y, preferred_element_type=F32)


def kernel(
    blocks, group, sizes,
    skip_ref, value_hbm, gate_hbm, filter_hbm, old_hbm, new_hbm,
    first_hbm, last_hbm, fwd_hbm, inv_hbm, turn_hbm, edge_hbm,
    mixed_hbm, sums_hbm, partner_hbm, out_ref,
    value_ref, gate_ref, filter_ref, old_ref, new_ref,
    first_ref, last_ref, fwd_ref, inv_ref, turn_ref, edge_ref,
    send_v, send_g, got_v, got_g, send_o, got_o, send_f, got_f, send_f2, got_f2,
    wide, lanes, turned, back, conv, edges, sums, route_row, route_ref,
    load_sem, send_sem, recv_sem,
):
    me = lax.axis_index("ctx")
    half = lax.axis_index("dp")
    rows, channels = value_ref.shape
    per_tile = 128 // group
    nz, ny, nx, nc = sizes
    low = ny * nx * nc

    loads = [
        pltpu.make_async_copy(src, dst, load_sem.at[i])
        for i, (src, dst) in enumerate([
            (value_hbm, value_ref), (filter_hbm, filter_ref), (gate_hbm, gate_ref),
            (old_hbm, old_ref), (new_hbm, new_ref), (first_hbm, first_ref), (last_hbm, last_ref),
            (turn_hbm, turn_ref), (edge_hbm, edge_ref), (fwd_hbm, fwd_ref), (inv_hbm, inv_ref),
        ])
    ]
    for load in loads:
        load.start()

    barrier = pltpu.get_barrier_semaphore()

    def greet(k, carry):
        pl.semaphore_signal(
            barrier, inc=1, device_id={"ctx": lax.rem(me + blocks // 2 + blocks - k, blocks)}, device_id_type=MESH
        )
        return carry

    lax.fori_loop(0, blocks // 2, greet, 0, unroll=8)
    lax.fori_loop(blocks // 2 + 1, blocks, greet, 0, unroll=8)
    pl.semaphore_signal(barrier, inc=1, device_id={"dp": 1 - half}, device_id_type=MESH)

    z, y, x, c = me // low, (me // (nx * nc)) % ny, (me // nc) % nx, me % nc
    heights = [((z + dz) % nz) * low for dz in range(nz)]

    def each_peer(act):
        steps = (4, 3, 5, 2, 6, 1, 7, 0)

        def turn_of(i, carry):
            r = low - 1 - i
            dc = r % nc
            dy = (r // nc) % ny
            dx = r // (ny * nc)
            place = (((y + dy) % ny) * nx + (x + dx) % nx) * nc + (c + dc) % nc
            for dz in steps:
                act(heights[dz] + place)
            return carry

        lax.fori_loop(0, low - 1, turn_of, 0)
        for dz in steps[:-1]:
            act(heights[dz] + me % low)

    def remote(src, dst, index, to):
        return pltpu.make_async_remote_copy(
            src_ref=src, dst_ref=dst, send_sem=send_sem.at[index], recv_sem=recv_sem.at[index],
            device_id=to, device_id_type=MESH,
        )

    def all_of(src, dst, index):
        rest = pl.ds(0, blocks - 1)
        return remote(src.at[rest], dst.at[rest], index, {"dp": 1 - half})

    def prepare(ref, send):
        for tile in range(channels // 128):
            to = slice(tile * per_tile, tile * per_tile + per_tile)
            piece = transposed(ref[:, tile * 128:(tile + 1) * 128])
            send[to] = piece.astype(BF16).reshape(per_tile, group, rows)

    loads[0].wait()
    prepare(value_ref, send_v)
    got_v[me] = send_v[me]
    loads[1].wait()
    here = me % low
    wide[:blocks] = transposed(filter_ref[...])
    for place in range(low):
        send_f[place * nz:(place + 1) * nz] = wide[pl.ds(place, nz, stride=low), :]

    def of_place(ref, place):
        return ref.at[pl.ds(pl.multiple_of(place * nz, nz), nz)]

    own = pl.ds(pl.multiple_of(here * nz, nz), nz)
    got_f[own, :] = send_f[own, :]

    pl.semaphore_wait(barrier, blocks)

    for step in range(1, low):
        place = (here + step) % low
        remote(of_place(send_f, place), of_place(got_f, here), 1, {"ctx": z * low + place}).start()
    each_peer(lambda to: remote(send_v.at[to], got_v.at[me], 0, {"ctx": to}).start())

    loads[2].wait()
    prepare(gate_ref, send_g)
    got_g[me] = send_g[me]
    rest = pl.ds(0, (low - 1) * nz)
    first_hop = remote(send_f.at[rest], got_f.at[rest], 1, {"dp": 1 - half})
    first_hop.wait_recv()
    for height in range(nz):
        send_f2[height] = got_f[pl.ds(height, low, stride=nz), :].astype(BF16)
    got_f2[z] = send_f2[z]
    for dz in range(1, nz):
        height = (z + dz) % nz
        remote(send_f2.at[height], got_f2.at[z], 5, {"ctx": height * low + here}).start()
    rest = pl.ds(0, nz - 1)
    second_hop = remote(send_f2.at[rest], got_f2.at[rest], 5, {"dp": 1 - half})
    each_peer(lambda to: remote(send_g.at[to], got_g.at[me], 2, {"ctx": to}).start())

    for load in loads[3:]:
        load.wait()

    spot = lax.broadcasted_iota(jnp.int32, (blocks, blocks), 0)
    hot_old = jnp.where(old_ref[...] == spot, 1.0, 0.0).astype(BF16)
    hot_new = jnp.where(new_ref[...] == spot, 1.0, 0.0).astype(BF16)
    first_slots = lax.dot_general(
        first_ref[...], hot_old, (((1,), (1,)), ((), ())), preferred_element_type=F32
    ).astype(BF16)
    last_slots = dot(hot_new, beside(last_ref)).astype(BF16)

    column = jnp.sum(jnp.where(new_ref[...] == spot, old_ref[...], 0), axis=1, keepdims=True)
    other = lax.broadcasted_iota(jnp.int32, (blocks, blocks), 1)
    row = jnp.sum(jnp.where(spot == other, column, 0), axis=0, keepdims=True)
    route_row[...] = jnp.broadcast_to(row, route_row.shape)
    routed = pltpu.make_async_copy(route_row, route_ref, load_sem.at[len(loads)])
    routed.start()

    turn_re, turn_im = turn_ref[0], turn_ref[1]
    edge_re, edge_im = edge_ref[0:1], edge_ref[1:2]
    top = lax.broadcasted_iota(jnp.int32, (blocks, rows), 0) == 0

    def turn(part, unit):
        part = part.astype(BF16).astype(F32)
        re, im = part[:blocks], part[blocks:]
        edges[pl.ds(unit, 1), :] = im[0:1]
        im = jnp.where(top, 0.0, im)
        at = pl.ds(unit * blocks, blocks)
        turned[at, :rows] = (turn_re * re - turn_im * im).astype(BF16)
        turned[at, rows:] = (turn_re * im + turn_im * re).astype(BF16)

    edges[...] = jnp.zeros_like(edges)
    all_of(send_v, got_v, 0).wait_recv()
    wide[...] = got_v[...].astype(F32).reshape(blocks * group, rows)
    for h in range(group):
        lanes[:, h * rows:(h + 1) * rows] = wide[pl.ds(h, blocks, stride=group), :].astype(BF16)
    for h in range(0, group, 2):
        part = dot(first_slots, lanes[:, h * rows:(h + 2) * rows])
        turn(part[:, :rows], h)
        turn(part[:, rows:], h + 1)
    second_hop.wait_recv()
    taps = got_f2[...].reshape(blocks, rows)
    turn(dot(first_ref[...], taps), group)

    fwd = beside(fwd_ref)
    inv = beside(inv_ref)
    filt = dot(turned[group * blocks:(group + 1) * blocks], fwd)
    filt_re, filt_im = filt[:, :rows], filt[:, rows:]
    line = edges[...]
    edge_spec = dot(
        jnp.concatenate([(edge_re * line).astype(BF16), (edge_im * line).astype(BF16)], axis=1), fwd
    )

    def multiplied(spec, fre, fim):
        re, im = spec[:, :rows], spec[:, rows:]
        return jnp.concatenate(
            [(re * fre - im * fim).astype(BF16), (re * fim + im * fre).astype(BF16)], axis=1
        )

    edge_filt = edge_spec[group:group + 1]
    edge_inner = dot(multiplied(edge_spec, edge_filt[:, :rows], edge_filt[:, rows:]), inv)
    edges[...] = edge_re * edge_inner[:, :rows] + edge_im * edge_inner[:, rows:]

    for h in range(0, group, 2):
        spec = dot(turned[h * blocks:(h + 2) * blocks], fwd)
        prod = jnp.concatenate(
            [multiplied(spec[:blocks], filt_re, filt_im), multiplied(spec[blocks:], filt_re, filt_im)],
            axis=0,
        )
        inner = dot(prod, inv)
        for i in range(2):
            re = inner[i * blocks:(i + 1) * blocks, :rows]
            im = inner[i * blocks:(i + 1) * blocks, rows:]
            back_im = jnp.where(top, edges[h + i:h + i + 1, :], turn_re * im - turn_im * re)
            at = slice(i * rows, (i + 1) * rows)
            back[:blocks, at] = (turn_re * re + turn_im * im).astype(BF16)
            back[blocks:, at] = back_im.astype(BF16)
        mixed = dot(last_slots, back[...])
        conv[pl.ds(h, blocks, stride=group), :] = mixed[:, :rows]
        conv[pl.ds(h + 1, blocks, stride=group), :] = mixed[:, rows:]

    sublane = lax.broadcasted_iota(jnp.int32, (group, rows), 0)
    skips = jnp.zeros((group, rows), F32)
    for h in range(group):
        skips = jnp.where(sublane == h, skip_ref[me * group + h], skips)

    routed.wait()
    all_of(send_g, got_g, 2).wait_recv()

    def gate(to):
        slot = route_ref[0, to]
        tile = conv[pl.ds(pl.multiple_of(to * group, group), group), :]
        values = got_v[slot].astype(F32)
        return (got_g[slot].astype(F32) * (tile + skips * values)).astype(BF16)

    def send_out(to):
        send_o[to] = gate(to)
        remote(send_o.at[to], got_o.at[me], 3, {"ctx": to}).start()

    got_o[me] = gate(me)
    each_peer(send_out)
    all_of(send_o, got_o, 3).wait_recv()

    square_sums = [jnp.zeros((8, rows), F32) for _ in range(4)]
    for slot in range(0, blocks, 2):
        pieces = got_o[slot:slot + 2].astype(F32).reshape(4, 8, rows)
        square_sums = [square_sums[i] + pieces[i] * pieces[i] for i in range(4)]
    total = square_sums[0] + square_sums[1] + (square_sums[2] + square_sums[3])
    sums[...] = jnp.broadcast_to(jnp.sum(total, axis=0, keepdims=True), sums.shape)
    swap = remote(sums, partner_hbm, 4, {"dp": 1 - half})
    swap.start()
    keep = pltpu.make_async_copy(sums, sums_hbm, load_sem.at[len(loads) + 1])
    keep.start()
    stores = []
    for i in range(2):
        for tile in range(i * channels // 256, (i + 1) * channels // 256):
            piece = got_o[tile * per_tile:(tile + 1) * per_tile].reshape(128, rows)
            out_ref[:, tile * 128:(tile + 1) * 128] = transposed(piece).astype(BF16)
        at = slice(i * channels // 2, (i + 1) * channels // 2)
        stores.append(
            pltpu.make_async_copy(out_ref.at[:, at], mixed_hbm.at[:, at], load_sem.at[len(loads) + 2 + i])
        )
        stores[-1].start()
    keep.wait()
    for store in stores:
        store.wait()
    swap.wait()
    all_of(send_v, got_v, 0).wait_send()
    first_hop.wait_send()
    second_hop.wait_send()
    all_of(send_g, got_g, 2).wait_send()
    all_of(send_o, got_o, 3).wait_send()


def scaled(whole, sums_hbm, partner_hbm, mixed_hbm, out_hbm, sums, mixed, out, in_sem, out_sem):
    rows = mixed.shape[0]
    part = rows // PARTS
    parts = [slice(i * part, (i + 1) * part) for i in range(PARTS)]
    ways = [(sums_hbm, sums.at[0]), (partner_hbm, sums.at[1])]
    ways += [(mixed_hbm.at[at], mixed.at[at]) for at in parts]
    loads = [pltpu.make_async_copy(src, dst, in_sem.at[i]) for i, (src, dst) in enumerate(ways)]
    for load in loads:
        load.start()
    for load in loads[:2]:
        load.wait()
    scale = lax.rsqrt((sums[0] + sums[1]) / whole + 1e-05).T[:, 0:1]
    stores = []
    for i, at in enumerate(parts):
        loads[2 + i].wait()
        out[at] = (mixed[at].astype(F32) * scale[at]).astype(BF16)
        stores.append(pltpu.make_async_copy(out.at[at], out_hbm.at[at], out_sem.at[i]))
        stores[-1].start()
    for store in stores:
        store.wait()


def body(sizes, value_rows, gate_rows, filter_rows, skip, old_owner, new_owner):
    blocks = lax.axis_size("ctx")
    rows, channels = value_rows.shape
    group = channels // blocks
    tables = [jnp.asarray(t) for t in make_tables(blocks, rows)]
    hbm = pl.BlockSpec(memory_space=pltpu.HBM)
    smem = pl.BlockSpec(memory_space=pltpu.SMEM)
    slots = pltpu.VMEM((blocks, group, rows), BF16)
    lines = pltpu.VMEM((blocks, rows), F32)
    ring = pltpu.VMEM((sizes[0], blocks // sizes[0], rows), BF16)
    owners = (old_owner.reshape(1, blocks), new_owner.reshape(1, blocks))
    arrays = (value_rows, gate_rows, filter_rows, *owners, *tables)
    loaded = [pltpu.VMEM(t.shape, t.dtype) for t in arrays]
    slab = pltpu.VMEM((rows, channels), BF16)
    sums = jax.ShapeDtypeStruct((8, rows), F32)
    mixed, own_sums, partner_sums = pl.pallas_call(
        functools.partial(kernel, blocks, group, sizes),
        out_shape=[jax.ShapeDtypeStruct((rows, channels), BF16), sums, sums],
        in_specs=[smem] + [hbm] * len(arrays),
        out_specs=[hbm] * 3,
        scratch_shapes=[slab] + loaded + [
            slots, slots, slots, slots, slots, slots, lines, lines, ring, ring,
            pltpu.VMEM((blocks * group, rows), F32),
            pltpu.VMEM((blocks, group * rows), BF16),
            pltpu.VMEM(((group + 1) * blocks, 2 * rows), BF16),
            pltpu.VMEM((2 * blocks, 2 * rows), BF16),
            pltpu.VMEM((blocks * group, rows), F32),
            pltpu.VMEM((group + 16, rows), F32),
            pltpu.VMEM((8, rows), F32),
            pltpu.VMEM((8, blocks), jnp.int32),
            pltpu.SMEM((8, blocks), jnp.int32),
            pltpu.SemaphoreType.DMA((len(arrays) + 4,)),
            pltpu.SemaphoreType.DMA((6,)),
            pltpu.SemaphoreType.DMA((6,)),
        ],
        compiler_params=pltpu.CompilerParams(
            collective_id=0, has_side_effects=True, vmem_limit_bytes=64 << 20
        ),
    )(skip, *arrays)
    return pl.pallas_call(
        functools.partial(scaled, channels * lax.axis_size("dp")),
        out_shape=jax.ShapeDtypeStruct((rows, channels), BF16),
        in_specs=[hbm] * 3,
        out_specs=hbm,
        scratch_shapes=[
            pltpu.VMEM((2, 8, rows), F32), slab, slab,
            pltpu.SemaphoreType.DMA((PARTS + 2,)),
            pltpu.SemaphoreType.DMA((PARTS,)),
        ],
        compiler_params=pltpu.CompilerParams(vmem_limit_bytes=64 << 20),
    )(own_sums, partner_sums, mixed)


def solution(mesh):
    placed = (P("ctx", "dp"), P("ctx", "dp"), P("ctx", "dp"), P("dp"), P(), P())
    sizes = (8, 4, 2, 2)
    return jax.shard_map(
        functools.partial(body, sizes), mesh=mesh, in_specs=placed, out_specs=P("ctx", "dp"), check_vma=False
    )
```
